128 devices in a mesh: tm: 2 (over x_lo), space: 64 (over y, z, x_hi, core).
Axes of the slice: x: 4 (x_hi: 2, x_lo: 2; x = x_hi * 2 + x_lo), y: 4, z: 4, core: 2. Of those that a mesh axis runs over, the one named last changes fastest.
Arguments:
- initial: float32 [2, 128, 128, 128], P(None, 'space'), may hold values from 0 to 1
- kappa: float32 [128, 128, 128], P('space'), may hold values from 0.1 to 1
Outputs:
- ends: float32 [2, 2, 128, 128, 128], P('tm', None, 'space')
The draws below stay inside these ranges and needn't reach their ends.
All inputs are finite; a program needn't handle non-finite values.
Results may differ from the reference program's by a relative error of at most 0.0001.
Values sent between devices are 32-bit elements; how exact they have to be, the bound alone decides.
A program may use at most 128 MiB of HBM per device.

```python
import math
import jax
import jax.numpy as jnp

SIDE = 128
ITERS = 2
NZ = 128
N_TM = 2


def shard_levels(own_key, dims, shards, least, high):
    def one(axis_at, blocks):
        steps = jax.random.uniform(jax.random.fold_in(jax.random.fold_in(own_key, 6), axis_at), (blocks,), jnp.float32, least / len(shards), high / len(shards))
        return jnp.repeat(jnp.exp(steps), dims[axis_at] // blocks).reshape((-1,) + (1,) * (len(dims) - axis_at - 1))

    gain = one(*shards[0])
    for cut in shards[1:]:
        gain = gain * one(*cut)
    return gain


def setup_inputs(seed: int = 0) -> dict:
    keys = jax.random.split(jax.random.key(seed), 3)
    initial = jnp.clip(1.0 * jax.random.uniform(keys[0], (2, NZ, SIDE, SIDE), jnp.float32) ** shard_levels(keys[0], (2, NZ, SIDE, SIDE), ((1, 64),), -0.2, 0.2), 0.0, 1.0)
    kappa = jnp.clip(jnp.exp(math.log(1.0) - 2.3025851 * jax.random.uniform(keys[1], (NZ, SIDE, SIDE), jnp.float32) ** shard_levels(keys[1], (NZ, SIDE, SIDE), ((0, 64),), -0.2, 0.2)), 0.1, 1.0)
    return dict(initial=initial, kappa=kappa)


STEP = 0.25
HALF = 0.125
FEED = 0.04
KILL = 0.06
WEIGHTS = ((5.0 / 24.0, 1.0 / 3.0, -1.0 / 24.0), (-1.0 / 24.0, 1.0 / 3.0, 5.0 / 24.0))


def react(padded, kappa, spacing):
    widths = [(0, 0)] * (padded.ndim - 2) + [(1, 1), (1, 1)]
    full = jnp.pad(padded, widths)
    centre = full[..., 1:-1, 1:-1, 1:-1]
    near = full[..., 2:, 1:-1, 1:-1] + full[..., :-2, 1:-1, 1:-1]
    near = near + full[..., 1:-1, 2:, 1:-1] + full[..., 1:-1, :-2, 1:-1]
    near = near + full[..., 1:-1, 1:-1, 2:] + full[..., 1:-1, 1:-1, :-2]
    laplace = (near - 6.0 * centre) / (spacing * spacing)
    first = centre[..., 0, :, :, :]
    second = centre[..., 1, :, :, :]
    source = first * second * second
    rate_a = kappa * laplace[..., 0, :, :, :] - source + FEED * (1.0 - first)
    rate_b = 0.5 * kappa * laplace[..., 1, :, :, :] + source - (FEED + KILL) * second
    return jnp.stack([rate_a, rate_b], axis=-4)


def restrict(field):
    shape = field.shape
    lead = shape[:-3]
    blocks = field.reshape(lead + (shape[-3] // 2, 2, shape[-2] // 2, 2, shape[-1] // 2, 2))
    return 0.125 * jnp.sum(blocks, axis=(-5, -3, -1))


def prolong(field):
    return jnp.repeat(jnp.repeat(jnp.repeat(field, 2, axis=-3), 2, axis=-2), 2, axis=-1)


def whole_rate(state, kappa, spacing):
    padded = jnp.pad(state, ((0, 0), (1, 1), (0, 0), (0, 0)))
    return react(padded, kappa, spacing)


def integrate(rates, row):
    return STEP * (WEIGHTS[row][0] * rates[0] + WEIGHTS[row][1] * rates[1] + WEIGHTS[row][2] * rates[2])


def reference(initial, kappa):
    coarse_kappa = restrict(kappa)
    coarse_initial = restrict(initial)
    nodes = [[initial, initial, initial] for slice_id in range(N_TM)]
    starts = [initial for slice_id in range(N_TM)]
    for step in range(ITERS):
        if step > 0:
            starts = [initial] + [nodes[slice_id - 1][2] for slice_id in range(1, N_TM)]
        carried = coarse_initial
        updated = []
        for slice_id in range(N_TM):
            old = [whole_rate(node, kappa, 1.0) for node in nodes[slice_id]]
            values = [starts[slice_id]]
            rates = []
            for row in range(2):
                rates.append(whole_rate(values[row], kappa, 1.0))
                values.append(values[row] + HALF * (rates[row] - old[row]) + integrate(old, row))
            rates.append(whole_rate(values[2], kappa, 1.0))
            coarse_w = [restrict(value) for value in values]
            folded = [restrict(integrate(rates, row)) for row in range(2)]
            coarse = [carried]
            for row in range(2):
                coarse.append(coarse[row] + HALF * (whole_rate(coarse[row], coarse_kappa, 2.0) - whole_rate(coarse_w[row], coarse_kappa, 2.0)) + folded[row])
            carried = coarse[2]
            updated.append([values[row] + prolong(coarse[row] - coarse_w[row]) for row in range(3)])
        nodes = updated
    return jnp.stack([nodes[slice_id][2] for slice_id in range(N_TM)])
```

```python
import functools

import jax
import jax.numpy as jnp
from jax import lax
from jax.experimental import pallas as pl
from jax.experimental.pallas import tpu as pltpu
from jax.sharding import PartitionSpec as P

MESH = pl.DeviceIdType.MESH
F32 = jnp.float32
STEP = 0.25
HALF = 0.125
FEED = 0.04
KILL = 0.06
S0 = (STEP * 5.0 / 24.0, STEP / 3.0, -STEP / 24.0)
S1 = (-STEP / 24.0, STEP / 3.0, STEP * 5.0 / 24.0)
N_COPIES = 48


def iota(dim):
    return lax.broadcasted_iota(jnp.int32, (64, 128), dim)


def even_lane():
    return iota(1) % 2 == 0


def beside_lanes(x, by):
    lane = iota(1)
    low = jnp.where(lane < by, 0.0, pltpu.roll(x, by, 1))
    high = jnp.where(lane >= 128 - by, 0.0, pltpu.roll(x, 128 - by, 1))
    return low + high


def row_above(x):
    return jnp.where(iota(0) == 0, 0.0, pltpu.roll(x, 1, 0))


def row_below(x):
    return jnp.where(iota(0) == 63, 0.0, pltpu.roll(x, 63, 0))


def fine_rate(buf, kn, p):
    centre = [[buf[p, sp, par] for par in range(2)] for sp in range(2)]
    kappa = [kn[p - 1, pl.ds(par, 64, stride=2), :] for par in range(2)]
    lap = []
    for sp in range(2):
        e, o = centre[sp]
        le = buf[p - 1, sp, 0] + buf[p + 1, sp, 0] + o + row_above(o) + beside_lanes(e, 1) - 6.0 * e
        lo = buf[p - 1, sp, 1] + buf[p + 1, sp, 1] + e + row_below(e) + beside_lanes(o, 1) - 6.0 * o
        lap.append((le, lo))
    out = [[None, None], [None, None]]
    for par in range(2):
        u, v = centre[0][par], centre[1][par]
        r = u * v * v
        out[0][par] = kappa[par] * lap[0][par] - r + FEED * (1.0 - u)
        out[1][par] = (0.5 * kappa[par]) * lap[1][par] + r - (FEED + KILL) * v
    return out


def each():
    return [(sp, par) for sp in range(2) for par in range(2)]


def pairs(su, sv):
    return jnp.where(even_lane(), su + pltpu.roll(su, 127, 1), sv + pltpu.roll(sv, 1, 1))


def restrict(buf, a, b):
    s = [buf[a, sp, 0] + buf[a, sp, 1] + buf[b, sp, 0] + buf[b, sp, 1] for sp in range(2)]
    return 0.125 * pairs(s[0], s[1])


def prolong(d):
    even = even_lane()
    return jnp.where(even, d, pltpu.roll(d, 1, 1)), jnp.where(even, pltpu.roll(d, 127, 1), d)


def local_rate(c):
    even = even_lane()
    u, v = prolong(c)
    r = u * v * v
    return jnp.where(even, -r, r) - jnp.where(even, FEED, FEED + KILL) * c


def coarse_lap(below, d, above):
    return below + above + row_above(d) + row_below(d) + beside_lanes(d, 2) - 6.0 * d


def kernel(
    n, init_ref, kap_ref, out_ref,
    nat, kn, x0, x1, x2, f0, tq0, tq1, u0, u1, u2, y, base, g0, ex, v1p, v2p,
    d1c, b2c, kc, wi, wpk, d11c, b11c, dd0, dd1, dd2, ddy, d5, c5, c5own, w0p, a1p, w1p,
    lsem, ssem, rsem,
):
    me = lax.axis_index("space")
    t = lax.axis_index("tm")
    c = lax.rem(me, 2)
    partner = me + 1 - 2 * c
    outer = me - 1 + 2 * c
    far_in = me + 2 - 4 * c
    far_out = me - 2 + 4 * c
    has_out = jnp.logical_and(outer >= 0, outer < n)
    has_far = jnp.logical_and(far_in >= 0, far_in < n)
    always = None
    first, second = t == 0, t == 1
    m_out = jnp.where(has_out, 1.0, 0.0).astype(F32)

    def when(cond, fn):
        if cond is None:
            fn()
        else:
            pl.when(cond)(fn)

    def both(a, b):
        if a is None:
            return b
        return a if b is None else jnp.logical_and(a, b)

    copies = []

    def copy(src, dst, tm, space, cond, back="same"):
        i = len(copies)
        cp = pltpu.make_async_remote_copy(
            src_ref=src, dst_ref=dst, send_sem=ssem.at[i], recv_sem=rsem.at[i],
            device_id=(tm, space), device_id_type=MESH)
        copies.append((cond, cp))
        return cond, cond if isinstance(back, str) else back, cp

    def start(*cs):
        for cond, _, cp in cs:
            when(cond, cp.start)

    def arrived(*cs):
        for _, back, cp in cs:
            when(back, cp.wait_recv)

    locals_ = [
        pltpu.make_async_copy(init_ref.at[:, 1 - c], nat.at[1], lsem.at[0]),
        pltpu.make_async_copy(init_ref.at[:, c], nat.at[2], lsem.at[1]),
        pltpu.make_async_copy(kap_ref.at[1 - c], kn.at[0], lsem.at[2]),
        pltpu.make_async_copy(kap_ref.at[c], kn.at[1], lsem.at[3]),
    ]
    for cp in locals_:
        cp.start()

    barrier = pltpu.get_barrier_semaphore()
    around = [(always, partner), (has_out, outer), (has_far, far_in), (has_out, far_out)]
    greet = [(t, cond, s) for cond, s in around] + [(1 - t, cond, s) for cond, s in [(always, me)] + around]
    for tm, cond, s in greet:
        when(cond, lambda tm=tm, s=s: pl.semaphore_signal(barrier, inc=1, device_id=(tm, s), device_id_type=MESH))

    @pl.when(jnp.logical_not(has_out))
    def _():
        zero_plane = jnp.zeros((2, 2, 64, 128), F32)
        for buf in (x1, x2):
            buf[4] = zero_plane
        v2p[3] = zero_plane
        nat[3] = jnp.zeros((2, 128, 128), F32)
        nat[4] = jnp.zeros((2, 128, 128), F32)
        kn[2] = jnp.zeros((128, 128), F32)
        zero = jnp.zeros((64, 128), F32)
        for buf in (d1c, d11c, c5, w0p):
            buf[3] = zero
            buf[4] = zero
        for buf in (b2c, kc, b11c, d5, a1p, w1p):
            buf[2] = zero

    @pl.when(jnp.logical_not(has_far))
    def _():
        zero = jnp.zeros((64, 128), F32)
        for buf in (d1c, d11c, c5, w0p):
            buf[0] = zero

    pl.semaphore_wait(barrier, 3 + 4 * has_out.astype(jnp.int32) + 2 * has_far.astype(jnp.int32))

    p_init = copy(init_ref.at[:, 1 - c], nat.at[0], t, partner, always)
    o_init = copy(init_ref.at[:, c], nat.at[3], t, outer, has_out)
    o_kap = copy(kap_ref.at[c], kn.at[2], t, outer, has_out)
    o_init2 = copy(init_ref.at[:, 1 - c], nat.at[4], t, outer, has_out)
    start(p_init, o_init, o_kap, o_init2)

    def convert(p):
        for sp, par in each():
            x0[p, sp, par] = nat[p, sp, pl.ds(par, 64, stride=2), :]

    for cp in locals_:
        cp.wait()
    convert(1)
    convert(2)
    ks = (kn[0, pl.ds(0, 64, stride=2), :] + kn[0, pl.ds(1, 64, stride=2), :]
          + kn[1, pl.ds(0, 64, stride=2), :] + kn[1, pl.ds(1, 64, stride=2), :])
    kc[1] = (0.125 * HALF / 4.0) * pairs(ks, 0.5 * ks)
    p_kc = copy(kc.at[1], kc.at[0], t, partner, always)
    o_kc = copy(kc.at[1], kc.at[2], t, outer, has_out)

    def masked(p):
        return jnp.where(p == 3, m_out, 1.0).astype(F32)

    def loop(lo, hi, body):
        def step(i, carry):
            body(i)
            return carry
        lax.fori_loop(lo, hi, step, 0)

    p_v1 = copy(x1.at[1], x1.at[0], t, partner, always)
    o_v1 = copy(x1.at[1], x1.at[4], t, outer, has_out)
    p_v2 = copy(x2.at[1], x2.at[0], t, partner, always)
    o_v2 = copy(x2.at[1], x2.at[4], t, outer, has_out)

    arrived(p_init)
    convert(0)

    def body_a1(p):
        @pl.when(p == 2)
        def _():
            arrived(o_init, o_kap, o_init2)
            convert(3)
            convert(4)

        f = fine_rate(x0, kn, p)
        m = masked(p)
        for sp, par in each():
            f0[p - 1, sp, par] = f[sp][par]
            x1[p, sp, par] = (x0[p, sp, par] + HALF * f[sp][par]) * m

        @pl.when(p == 1)
        def _():
            start(p_v1, o_v1, p_kc, o_kc)

    loop(1, 4, body_a1)

    def body_a2(p):
        @pl.when(p == 1)
        def _():
            arrived(p_v1)

        @pl.when(p == 3)
        def _():
            arrived(o_v1)

        g = fine_rate(x1, kn, p)
        m = masked(p)
        for sp, par in each():
            r, f = g[sp][par], f0[p - 1, sp, par]
            x2[p, sp, par] = (x1[p, sp, par] + HALF * r) * m
            tq0[p - 1, sp, par] = S0[0] * f + S0[1] * r
            tq1[p - 1, sp, par] = S1[0] * f + S1[1] * r

        @pl.when(p == 1)
        def _():
            start(p_v2, o_v2)

    loop(1, 4, body_a2)

    def add_last(buf, p):
        g = fine_rate(buf, kn, p)
        for sp, par in each():
            tq0[p - 1, sp, par] = tq0[p - 1, sp, par] + S0[2] * g[sp][par]
            tq1[p - 1, sp, par] = tq1[p - 1, sp, par] + S1[2] * g[sp][par]

    def body_a3(i):
        p = 2 - i

        @pl.when(p == 1)
        def _():
            arrived(p_v2)

        add_last(x2, p)

    loop(0, 2, body_a3)

    w0, w1, w2 = (restrict(x, 1, 2) for x in (x0, x1, x2))
    q0, q1 = restrict(tq0, 0, 1), restrict(tq1, 0, 1)
    c1 = w0 + q0
    d1c[2] = c1 - w1
    b2c[1] = c1 + q1 + HALF * (local_rate(c1) - local_rate(w1))
    wpk[0] = w0
    wpk[1] = w2

    def spread(buf, at, cond):
        return [
            copy(buf.at[at], buf.at[3], t, outer, both(cond, has_out)),
            copy(buf.at[at], buf.at[4], t, far_in, both(cond, has_far), both(cond, has_out)),
            copy(buf.at[at], buf.at[0], t, far_out, both(cond, has_out), both(cond, has_far)),
            copy(buf.at[at], buf.at[1], t, partner, cond),
        ]

    def beside(buf, cond):
        return [
            copy(buf.at[1], buf.at[2], t, outer, both(cond, has_out)),
            copy(buf.at[1], buf.at[0], t, partner, cond),
        ]

    r2 = spread(d1c, 2, always) + beside(b2c, always) + [copy(wpk, wi, t, partner, always)]
    start(*r2)
    w0o = restrict(x0, 3, 4)
    arrived(p_kc, o_kc, o_v2)
    w2o = restrict(x2, 3, 4)
    arrived(*r2)
    w0s = (wi[0], w0, w0o)
    w2s = (wi[1], w2, w2o)

    def corrected(d, b, j):
        r = b[j] + kc[j] * coarse_lap(d[j], d[j + 1], d[j + 2])
        return r * m_out if j == 2 else r

    c02 = [corrected(d1c, b2c, j) for j in range(3)]
    for j in range(3):
        ddy[j] = c02[j] - w2s[j]

    @pl.when(first)
    def _():
        for j in range(3):
            dd1[j] = d1c[j + 1]
            dd2[j] = ddy[j]

    r3 = spread(d11c, 2, second) + beside(b11c, second)

    @pl.when(second)
    def _():
        d10 = [c02[j] - w0s[j] for j in range(3)]
        for j in range(3):
            dd0[j] = d10[j]
        c11 = c02[1] + q0 + kc[1] * coarse_lap(*d10) + HALF * (local_rate(c02[1]) - local_rate(w0))
        d11c[2] = c11 - w1
        b11c[1] = c11 + q1 + HALF * (local_rate(c11) - local_rate(w1))

    start(*r3)
    arrived(*r3)

    @pl.when(second)
    def _():
        for j in range(3):
            dd1[j] = d11c[j + 1]
            dd2[j] = corrected(d11c, b11c, j) - w2s[j]

    def add_prolonged(dst, src, dd, p):
        j = (p + 1) // 2
        up = prolong(dd[j])
        for sp, par in each():
            dst[p, sp, par] = src[p, sp, par] + up[sp]

    def body_u(p):
        add_prolonged(u1, x1, dd1, p)
        add_prolonged(u2, x2, dd2, p)

    loop(0, 5, body_u)

    @pl.when(first)
    def _():
        def body(p):
            for sp, par in each():
                g0[p - 1, sp, par] = f0[p - 1, sp, par]
                base[p - 1, sp, par] = x0[p, sp, par]
        loop(1, 4, body)

    @pl.when(second)
    def _():
        def body_uy(p):
            add_prolonged(u0, x0, dd0, p)
            add_prolonged(y, x2, ddy, p)
        loop(0, 5, body_uy)

        def body(p):
            f = fine_rate(u0, kn, p)
            r = fine_rate(y, kn, p)
            for sp, par in each():
                f0[p - 1, sp, par] = f[sp][par]
                g0[p - 1, sp, par] = r[sp][par]
                base[p - 1, sp, par] = y[p, sp, par] + HALF * (r[sp][par] - f[sp][par])
        loop(1, 4, body)

    p_v1p = copy(v1p.at[1], v1p.at[0], t, partner, always)
    p_v2p = copy(v2p.at[1], v2p.at[0], t, partner, always)
    o_v2p = copy(v2p.at[2], v2p.at[3], t, outer, has_out)

    def body_c1(p):
        fa = fine_rate(u1, kn, p)
        fb = fine_rate(u2, kn, p)
        m = masked(p)
        for sp, par in each():
            f, a, b = f0[p - 1, sp, par], fa[sp][par], fb[sp][par]
            v1p[p, sp, par] = (base[p - 1, sp, par] + S0[0] * f + S0[1] * a + S0[2] * b) * m
            ex[p - 1, sp, par] = S1[0] * f + (S1[1] - HALF) * a + S1[2] * b

        @pl.when(p == 1)
        def _():
            start(p_v1p)

    loop(1, 4, body_c1)

    def body_c2(i):
        p = 2 - i

        @pl.when(p == 1)
        def _():
            arrived(p_v1p)

        g = fine_rate(v1p, kn, p)
        for sp, par in each():
            r, z = g[sp][par], g0[p - 1, sp, par]
            v2p[p, sp, par] = v1p[p, sp, par] + ex[p - 1, sp, par] + HALF * r
            tq0[p - 1, sp, par] = S0[0] * z + S0[1] * r
            tq1[p - 1, sp, par] = S1[0] * z + S1[1] * r

        @pl.when(p == 2)
        def _():
            start(o_v2p)

        @pl.when(p == 1)
        def _():
            start(p_v2p)

    loop(0, 2, body_c2)

    def body_c3(p):
        @pl.when(p == 1)
        def _():
            arrived(p_v2p)

        @pl.when(p == 2)
        def _():
            arrived(o_v2p)

        add_last(v2p, p)

    loop(1, 3, body_c3)

    w1, w2 = restrict(v1p, 1, 2), restrict(v2p, 1, 2)
    q0, q1 = restrict(tq0, 0, 1), restrict(tq1, 0, 1)

    r5 = beside(d5, first)
    r6 = [copy(c5own.at[0], c5.at[at], 1, s, both(first, cond), both(second, back))
          for at, cond, back, s in ((3, has_out, has_out, outer), (4, has_far, has_out, far_in),
                                    (0, has_out, has_far, far_out), (2, always, always, me),
                                    (1, always, always, partner))]
    r7 = spread(w0p, 2, second) + beside(a1p, second) + beside(w1p, second)

    @pl.when(first)
    def _():
        c1 = w0 + q0
        d5[1] = c1 - w1
        start(*r5)
        b = c1 + q1 + HALF * (local_rate(c1) - local_rate(w1))
        arrived(*r5)
        end = b + kc[1] * coarse_lap(d5[0], d5[1], d5[2])
        c5own[0] = end
        start(*r6)
        dd2[1] = end - w2

    @pl.when(second)
    def _():
        w0n = restrict(y, 1, 2)
        w0p[2] = w0n
        a1p[1] = q0 - HALF * local_rate(w0n)
        w1p[1] = w1
        start(*r7)
        arrived(*r7)

    arrived(*r6)

    @pl.when(second)
    def _():
        d10 = [c5[j] - w0p[j] for j in range(5)]
        c11 = []
        for j in range(3):
            r = c5[j + 1] + a1p[j] + kc[j] * coarse_lap(d10[j], d10[j + 1], d10[j + 2]) + HALF * local_rate(c5[j + 1])
            c11.append(r * m_out if j == 2 else r)
        d11 = [c11[j] - w1p[j] for j in range(3)]
        end = c11[1] + q1 + kc[1] * coarse_lap(*d11) + HALF * (local_rate(c11[1]) - local_rate(w1))
        dd2[1] = end - w2

    up = prolong(dd2[1])
    for p, plane in ((1, 1 - c), (2, c)):
        for sp, par in each():
            out_ref[0, sp, plane, pl.ds(par, 64, stride=2), :] = v2p[p, sp, par] + up[sp]

    for cond, cp in copies:
        when(cond, cp.wait_send)


def shards(n, initial, kappa):
    fine = lambda k: pltpu.VMEM((k, 2, 2, 64, 128), F32)
    coarse = lambda k: pltpu.VMEM((k, 64, 128), F32)
    return pl.pallas_call(
        functools.partial(kernel, n),
        out_shape=jax.ShapeDtypeStruct((1,) + initial.shape, F32),
        in_specs=[pl.BlockSpec(memory_space=pl.ANY)] * 2,
        out_specs=pl.BlockSpec(memory_space=pltpu.VMEM),
        scratch_shapes=[
            pltpu.VMEM((5, 2, 128, 128), F32), pltpu.VMEM((3, 128, 128), F32),
            fine(5), fine(5), fine(5), fine(3), fine(3), fine(3), fine(5), fine(5), fine(5), fine(5), fine(3), fine(3),
            fine(3), fine(4), fine(4),
            coarse(5), coarse(3), coarse(3), coarse(2), coarse(2), coarse(5), coarse(3), coarse(3), coarse(3), coarse(3),
            coarse(3), coarse(3), coarse(5), coarse(1), coarse(5), coarse(3), coarse(3),
            pltpu.SemaphoreType.DMA((4,)), pltpu.SemaphoreType.DMA((N_COPIES,)), pltpu.SemaphoreType.DMA((N_COPIES,)),
        ],
        compiler_params=pltpu.CompilerParams(
            collective_id=0, has_side_effects=True, vmem_limit_bytes=40 * 1024 * 1024),
    )(initial, kappa)


def solution(mesh):
    return jax.shard_map(
        functools.partial(shards, mesh.shape["space"]),
        mesh=mesh,
        in_specs=(P(None, "space", None, None), P("space", None, None)),
        out_specs=P("tm", None, "space", None, None),
        check_vma=False,
    )
```

```python
import functools

import jax
import jax.numpy as jnp
from jax import lax
from jax.experimental import pallas as pl
from jax.experimental.pallas import tpu as pltpu
from jax.sharding import PartitionSpec as P

MESH = pl.DeviceIdType.MESH
F32 = jnp.float32
STEP = 0.25
HALF = 0.125
FEED = 0.04
KILL = 0.06
S0 = (STEP * 5.0 / 24.0, STEP / 3.0, -STEP / 24.0)
S1 = (-STEP / 24.0, STEP / 3.0, STEP * 5.0 / 24.0)
N_COPIES = 48


def iota(dim):
    return lax.broadcasted_iota(jnp.int32, (64, 128), dim)


def even_lane():
    return iota(1) % 2 == 0


def beside_lanes(x, by):
    lane = iota(1)
    low = jnp.where(lane < by, 0.0, pltpu.roll(x, by, 1))
    high = jnp.where(lane >= 128 - by, 0.0, pltpu.roll(x, 128 - by, 1))
    return low + high


def row_above(x):
    return jnp.where(iota(0) == 0, 0.0, pltpu.roll(x, 1, 0))


def row_below(x):
    return jnp.where(iota(0) == 63, 0.0, pltpu.roll(x, 63, 0))


def fine_rate(buf, kn, p):
    centre = [[buf[p, sp, par] for par in range(2)] for sp in range(2)]
    kappa = [kn[p - 1, pl.ds(par, 64, stride=2), :] for par in range(2)]
    lap = []
    for sp in range(2):
        e, o = centre[sp]
        le = buf[p - 1, sp, 0] + buf[p + 1, sp, 0] + o + row_above(o) + beside_lanes(e, 1) - 6.0 * e
        lo = buf[p - 1, sp, 1] + buf[p + 1, sp, 1] + e + row_below(e) + beside_lanes(o, 1) - 6.0 * o
        lap.append((le, lo))
    out = [[None, None], [None, None]]
    for par in range(2):
        u, v = centre[0][par], centre[1][par]
        r = u * v * v
        out[0][par] = kappa[par] * lap[0][par] - r + FEED * (1.0 - u)
        out[1][par] = (0.5 * kappa[par]) * lap[1][par] + r - (FEED + KILL) * v
    return out


def each():
    return [(sp, par) for sp in range(2) for par in range(2)]


def pairs(su, sv):
    return jnp.where(even_lane(), su + pltpu.roll(su, 127, 1), sv + pltpu.roll(sv, 1, 1))


def restrict(buf, a, b):
    s = [buf[a, sp, 0] + buf[a, sp, 1] + buf[b, sp, 0] + buf[b, sp, 1] for sp in range(2)]
    return 0.125 * pairs(s[0], s[1])


def prolong(d):
    even = even_lane()
    return jnp.where(even, d, pltpu.roll(d, 1, 1)), jnp.where(even, pltpu.roll(d, 127, 1), d)


def local_rate(c):
    even = even_lane()
    u, v = prolong(c)
    r = u * v * v
    return jnp.where(even, -r, r) - jnp.where(even, FEED, FEED + KILL) * c


def coarse_lap(below, d, above):
    return below + above + row_above(d) + row_below(d) + beside_lanes(d, 2) - 6.0 * d


def kernel(
    n, init_ref, kap_ref, out_ref,
    nat, kn, x0, x1, x2, f0, tq0, tq1, u0, u1, u2, y, base, g0, ex, v1p, v2p,
    d1c, b2c, kc, wi, wpk, d11c, b11c, dd0, dd1, dd2, ddy, d5, c5, c5own, w0p, a1p, w1p, e3,
    lsem, ssem, rsem,
):
    me = lax.axis_index("space")
    t = lax.axis_index("tm")
    c = lax.rem(me, 2)
    partner = me + 1 - 2 * c
    outer = me - 1 + 2 * c
    far_in = me + 2 - 4 * c
    far_out = me - 2 + 4 * c
    has_out = jnp.logical_and(outer >= 0, outer < n)
    has_far = jnp.logical_and(far_in >= 0, far_in < n)
    always = None
    first, second = t == 0, t == 1
    m_out = jnp.where(has_out, 1.0, 0.0).astype(F32)

    def when(cond, fn):
        if cond is None:
            fn()
        else:
            pl.when(cond)(fn)

    def both(a, b):
        if a is None:
            return b
        return a if b is None else jnp.logical_and(a, b)

    copies = []

    def copy(src, dst, tm, space, cond, back="same"):
        i = len(copies)
        cp = pltpu.make_async_remote_copy(
            src_ref=src, dst_ref=dst, send_sem=ssem.at[i], recv_sem=rsem.at[i],
            device_id=(tm, space), device_id_type=MESH)
        copies.append((cond, cp))
        return cond, cond if isinstance(back, str) else back, cp

    def start(*cs):
        for cond, _, cp in cs:
            when(cond, cp.start)

    def arrived(*cs):
        for _, back, cp in cs:
            when(back, cp.wait_recv)

    locals_ = [
        pltpu.make_async_copy(init_ref.at[:, 1 - c], nat.at[1], lsem.at[0]),
        pltpu.make_async_copy(init_ref.at[:, c], nat.at[2], lsem.at[1]),
        pltpu.make_async_copy(kap_ref.at[1 - c], kn.at[0], lsem.at[2]),
        pltpu.make_async_copy(kap_ref.at[c], kn.at[1], lsem.at[3]),
    ]
    for cp in locals_:
        cp.start()

    barrier = pltpu.get_barrier_semaphore()
    around = [(always, partner), (has_out, outer), (has_far, far_in), (has_out, far_out)]
    greet = [(t, cond, s) for cond, s in around] + [(1 - t, cond, s) for cond, s in [(always, me)] + around]
    for tm, cond, s in greet:
        when(cond, lambda tm=tm, s=s: pl.semaphore_signal(barrier, inc=1, device_id=(tm, s), device_id_type=MESH))

    @pl.when(jnp.logical_not(has_out))
    def _():
        zero_plane = jnp.zeros((2, 2, 64, 128), F32)
        for buf in (x1, x2):
            buf[4] = zero_plane
        nat[3] = jnp.zeros((2, 128, 128), F32)
        nat[4] = jnp.zeros((2, 128, 128), F32)
        kn[2] = jnp.zeros((128, 128), F32)
        zero = jnp.zeros((64, 128), F32)
        for buf in (d1c, d11c, c5, w0p):
            buf[3] = zero
            buf[4] = zero
        for buf in (b2c, kc, b11c, d5, a1p, w1p):
            buf[2] = zero
        e3[1] = zero

    @pl.when(jnp.logical_not(has_far))
    def _():
        zero = jnp.zeros((64, 128), F32)
        for buf in (d1c, d11c, c5, w0p):
            buf[0] = zero
        e3[0] = zero

    v2p[3] = jnp.zeros((2, 2, 64, 128), F32)
    pl.semaphore_wait(barrier, 3 + 4 * has_out.astype(jnp.int32) + 2 * has_far.astype(jnp.int32))

    for cp in locals_:
        cp.wait()
    p_init = copy(nat.at[1], nat.at[0], t, partner, always)
    o_init = copy(nat.at[2], nat.at[3], t, outer, has_out)
    o_kap = copy(kn.at[1], kn.at[2], t, outer, has_out)
    o_init2 = copy(nat.at[1], nat.at[4], t, outer, has_out)
    start(p_init, o_init, o_kap, o_init2)

    def convert(p):
        for sp, par in each():
            x0[p, sp, par] = nat[p, sp, pl.ds(par, 64, stride=2), :]

    convert(1)
    convert(2)
    ks = (kn[0, pl.ds(0, 64, stride=2), :] + kn[0, pl.ds(1, 64, stride=2), :]
          + kn[1, pl.ds(0, 64, stride=2), :] + kn[1, pl.ds(1, 64, stride=2), :])
    kc[1] = (0.125 * HALF / 4.0) * pairs(ks, 0.5 * ks)
    p_kc = copy(kc.at[1], kc.at[0], t, partner, always)
    o_kc = copy(kc.at[1], kc.at[2], t, outer, has_out)

    def masked(p):
        return jnp.where(p == 3, m_out, 1.0).astype(F32)

    def loop(lo, hi, body):
        def step(i, carry):
            body(i)
            return carry
        lax.fori_loop(lo, hi, step, 0)

    p_v1 = copy(x1.at[1], x1.at[0], t, partner, always)
    o_v1 = copy(x1.at[1], x1.at[4], t, outer, has_out)
    p_v2 = copy(x2.at[1], x2.at[0], t, partner, always)
    o_v2 = copy(x2.at[1], x2.at[4], t, outer, has_out)

    arrived(p_init)
    convert(0)

    def body_a1(p):
        @pl.when(p == 2)
        def _():
            arrived(o_init, o_kap, o_init2)
            convert(3)
            convert(4)

        f = fine_rate(x0, kn, p)
        m = masked(p)
        for sp, par in each():
            f0[p - 1, sp, par] = f[sp][par]
            x1[p, sp, par] = (x0[p, sp, par] + HALF * f[sp][par]) * m

        @pl.when(p == 1)
        def _():
            start(p_v1, o_v1, p_kc, o_kc)

    loop(1, 4, body_a1)

    def body_a2(p):
        @pl.when(p == 1)
        def _():
            arrived(p_v1)

        @pl.when(p == 3)
        def _():
            arrived(o_v1)

        g = fine_rate(x1, kn, p)
        m = masked(p)
        for sp, par in each():
            r, f = g[sp][par], f0[p - 1, sp, par]
            x2[p, sp, par] = (x1[p, sp, par] + HALF * r) * m
            tq0[p - 1, sp, par] = S0[0] * f + S0[1] * r
            tq1[p - 1, sp, par] = S1[0] * f + S1[1] * r

        @pl.when(p == 1)
        def _():
            start(p_v2, o_v2)

    loop(1, 4, body_a2)

    def add_last(buf, p):
        g = fine_rate(buf, kn, p)
        for sp, par in each():
            tq0[p - 1, sp, par] = tq0[p - 1, sp, par] + S0[2] * g[sp][par]
            tq1[p - 1, sp, par] = tq1[p - 1, sp, par] + S1[2] * g[sp][par]

    def body_a3(i):
        p = 2 - i

        @pl.when(p == 1)
        def _():
            arrived(p_v2)

        add_last(x2, p)

    loop(0, 2, body_a3)

    w0, w1, w2 = (restrict(x, 1, 2) for x in (x0, x1, x2))
    q0, q1 = restrict(tq0, 0, 1), restrict(tq1, 0, 1)
    c1 = w0 + q0
    d1c[2] = c1 - w1
    b2c[1] = c1 + q1 + HALF * (local_rate(c1) - local_rate(w1))
    wpk[0] = w0
    wpk[1] = w2

    def spread(buf, at, cond):
        return [
            copy(buf.at[at], buf.at[3], t, outer, both(cond, has_out)),
            copy(buf.at[at], buf.at[4], t, far_in, both(cond, has_far), both(cond, has_out)),
            copy(buf.at[at], buf.at[0], t, far_out, both(cond, has_out), both(cond, has_far)),
            copy(buf.at[at], buf.at[1], t, partner, cond),
        ]

    def beside(buf, cond):
        return [
            copy(buf.at[1], buf.at[2], t, outer, both(cond, has_out)),
            copy(buf.at[1], buf.at[0], t, partner, cond),
        ]

    r2 = spread(d1c, 2, always) + beside(b2c, always) + [copy(wpk, wi, t, partner, always)]
    start(*r2)
    w0o = restrict(x0, 3, 4)
    arrived(p_kc, o_kc, o_v2)
    w2o = restrict(x2, 3, 4)
    arrived(*r2)
    w0s = (wi[0], w0, w0o)
    w2s = (wi[1], w2, w2o)

    def corrected(d, b, j):
        r = b[j] + kc[j] * coarse_lap(d[j], d[j + 1], d[j + 2])
        return r * m_out if j == 2 else r

    c02 = [corrected(d1c, b2c, j) for j in range(3)]
    for j in range(3):
        ddy[j] = c02[j] - w2s[j]

    @pl.when(first)
    def _():
        for j in range(3):
            dd1[j] = d1c[j + 1]
            dd2[j] = ddy[j]

    r3 = spread(d11c, 2, second) + beside(b11c, second)

    @pl.when(second)
    def _():
        d10 = [c02[j] - w0s[j] for j in range(3)]
        for j in range(3):
            dd0[j] = d10[j]
        c11 = c02[1] + q0 + kc[1] * coarse_lap(*d10) + HALF * (local_rate(c02[1]) - local_rate(w0))
        d11c[2] = c11 - w1
        b11c[1] = c11 + q1 + HALF * (local_rate(c11) - local_rate(w1))

    start(*r3)

    def add_prolonged(dst, src, dd, p):
        j = (p + 1) // 2
        up = prolong(dd[j])
        for sp, par in each():
            dst[p, sp, par] = src[p, sp, par] + up[sp]

    r7a = spread(w0p, 2, second)

    @pl.when(first)
    def _():
        def body(p):
            for sp, par in each():
                g0[p - 1, sp, par] = f0[p - 1, sp, par]
                base[p - 1, sp, par] = x0[p, sp, par]
        loop(1, 4, body)

    @pl.when(second)
    def _():
        def body_uy(p):
            add_prolonged(u0, x0, dd0, p)
            add_prolonged(y, x2, ddy, p)
        loop(0, 5, body_uy)
        w0p[2] = restrict(y, 1, 2)
        start(*r7a)

        def body(p):
            f = fine_rate(u0, kn, p)
            r = fine_rate(y, kn, p)
            for sp, par in each():
                f0[p - 1, sp, par] = f[sp][par]
                g0[p - 1, sp, par] = r[sp][par]
                base[p - 1, sp, par] = y[p, sp, par] + HALF * (r[sp][par] - f[sp][par])
        loop(1, 4, body)

    arrived(*r3)

    @pl.when(second)
    def _():
        for j in range(3):
            dd1[j] = d11c[j + 1]
            dd2[j] = corrected(d11c, b11c, j) - w2s[j]

    def body_u(p):
        add_prolonged(u1, x1, dd1, p)
        add_prolonged(u2, x2, dd2, p)

    loop(0, 5, body_u)

    p_v1p = copy(v1p.at[1], v1p.at[0], t, partner, always)
    p_v2p = copy(v2p.at[1], v2p.at[0], t, partner, always)
    r_e = [copy(e3.at[2], e3.at[1], t, outer, has_out), copy(e3.at[2], e3.at[0], t, far_out, has_out, has_far)]

    def body_c1(p):
        fa = fine_rate(u1, kn, p)
        fb = fine_rate(u2, kn, p)
        m = masked(p)
        for sp, par in each():
            f, a, b = f0[p - 1, sp, par], fa[sp][par], fb[sp][par]
            v1p[p, sp, par] = (base[p - 1, sp, par] + S0[0] * f + S0[1] * a + S0[2] * b) * m
            ex[p - 1, sp, par] = S1[0] * f + (S1[1] - HALF) * a + S1[2] * b

        @pl.when(p == 1)
        def _():
            start(p_v1p)

    loop(1, 4, body_c1)

    def body_c2(i):
        p = 2 - i

        @pl.when(p == 1)
        def _():
            arrived(p_v1p)

        g = fine_rate(v1p, kn, p)
        for sp, par in each():
            r, z = g[sp][par], g0[p - 1, sp, par]
            v2p[p, sp, par] = v1p[p, sp, par] + ex[p - 1, sp, par] + HALF * r
            tq0[p - 1, sp, par] = S0[0] * z + S0[1] * r
            tq1[p - 1, sp, par] = S1[0] * z + S1[1] * r

        @pl.when(p == 2)
        def _():
            k = [kn[2, pl.ds(par, 64, stride=2), :] for par in range(2)]
            su = k[0] * v2p[2, 0, 0] + k[1] * v2p[2, 0, 1]
            sv = k[0] * v2p[2, 1, 0] + k[1] * v2p[2, 1, 1]
            e3[2] = 0.125 * pairs(su, 0.5 * sv)
            start(*r_e)

        @pl.when(p == 1)
        def _():
            start(p_v2p)

    loop(0, 2, body_c2)

    def body_c3(i):
        p = 2 - i

        @pl.when(p == 1)
        def _():
            arrived(p_v2p)

        add_last(v2p, p)

    loop(0, 2, body_c3)

    w1, w2 = restrict(v1p, 1, 2), restrict(v2p, 1, 2)
    q0, q1 = restrict(tq0, 0, 1), restrict(tq1, 0, 1)

    r5 = beside(d5, first)
    r6 = [copy(c5own.at[0], c5.at[at], 1, s, both(first, cond), both(second, back))
          for at, cond, back, s in ((3, has_out, has_out, outer), (4, has_far, has_out, far_in),
                                    (0, has_out, has_far, far_out), (2, always, always, me),
                                    (1, always, always, partner))]
    r7 = beside(a1p, second) + beside(w1p, second)

    @pl.when(first)
    def _():
        d5[1] = w0 + q0 - w1
        start(*r5)

    @pl.when(second)
    def _():
        w1p[1] = w1
        a1p[1] = q0 - HALF * local_rate(w0p[2])
        start(*r7)

    arrived(*r_e)
    e_own = (S0[2] * e3[0], S0[2] * e3[1], S0[2] * e3[2])
    q0 = q0 + e_own[1]
    q1 = q1 + S1[2] * e3[1]

    @pl.when(first)
    def _():
        c1 = w0 + q0
        b = c1 + q1 + HALF * (local_rate(c1) - local_rate(w1))
        arrived(*r5)
        end = b + kc[1] * coarse_lap(d5[0] + e_own[0], c1 - w1, d5[2] + e_own[2])
        c5own[0] = end
        start(*r6)
        dd2[1] = end - w2

    arrived(*r7a)
    arrived(*r7)

    arrived(*r6)

    @pl.when(second)
    def _():
        d10 = [c5[j] - w0p[j] for j in range(5)]
        c11 = []
        for j in range(3):
            r = c5[j + 1] + (a1p[j] + e_own[j]) + kc[j] * coarse_lap(d10[j], d10[j + 1], d10[j + 2]) + HALF * local_rate(c5[j + 1])
            c11.append(r * m_out if j == 2 else r)
        d11 = [c11[j] - w1p[j] for j in range(3)]
        end = c11[1] + q1 + kc[1] * coarse_lap(*d11) + HALF * (local_rate(c11[1]) - local_rate(w1))
        dd2[1] = end - w2

    up = prolong(dd2[1])
    for p, plane in ((1, 1 - c), (2, c)):
        for sp, par in each():
            out_ref[0, sp, plane, pl.ds(par, 64, stride=2), :] = v2p[p, sp, par] + up[sp]

    for cond, cp in copies:
        when(cond, cp.wait_send)


def shards(n, initial, kappa):
    fine = lambda k: pltpu.VMEM((k, 2, 2, 64, 128), F32)
    coarse = lambda k: pltpu.VMEM((k, 64, 128), F32)
    return pl.pallas_call(
        functools.partial(kernel, n),
        out_shape=jax.ShapeDtypeStruct((1,) + initial.shape, F32),
        in_specs=[pl.BlockSpec(memory_space=pltpu.HBM)] * 2,
        out_specs=pl.BlockSpec(memory_space=pltpu.VMEM),
        scratch_shapes=[
            pltpu.VMEM((5, 2, 128, 128), F32), pltpu.VMEM((3, 128, 128), F32),
            fine(5), fine(5), fine(5), fine(3), fine(3), fine(3), fine(5), fine(5), fine(5), fine(5), fine(3), fine(3),
            fine(3), fine(4), fine(4),
            coarse(5), coarse(3), coarse(3), coarse(2), coarse(2), coarse(5), coarse(3), coarse(3), coarse(3), coarse(3),
            coarse(3), coarse(3), coarse(5), coarse(1), coarse(5), coarse(3), coarse(3), coarse(3),
            pltpu.SemaphoreType.DMA((4,)), pltpu.SemaphoreType.DMA((N_COPIES,)), pltpu.SemaphoreType.DMA((N_COPIES,)),
        ],
        compiler_params=pltpu.CompilerParams(
            collective_id=0, has_side_effects=True, vmem_limit_bytes=63 * 1024 * 1024),
    )(initial, kappa)


def solution(mesh):
    return jax.shard_map(
        functools.partial(shards, mesh.shape["space"]),
        mesh=mesh,
        in_specs=(P(None, "space", None, None), P("space", None, None)),
        out_specs=P("tm", None, "space", None, None),
        check_vma=False,
    )
```

```python
import functools

import jax
import jax.numpy as jnp
from jax import lax
from jax.experimental import pallas as pl
from jax.experimental.pallas import tpu as pltpu
from jax.sharding import PartitionSpec as P

MESH = pl.DeviceIdType.MESH
F32 = jnp.float32
STEP = 0.25
HALF = 0.125
FEED = 0.04
KILL = 0.06
S0 = (STEP * 5.0 / 24.0, STEP / 3.0, -STEP / 24.0)
S1 = (-STEP / 24.0, STEP / 3.0, STEP * 5.0 / 24.0)
N_COPIES = 48


def iota(dim):
    return lax.broadcasted_iota(jnp.int32, (64, 128), dim)


def even_lane():
    return iota(1) % 2 == 0


def beside_lanes(x, by):
    lane = iota(1)
    low = jnp.where(lane < by, 0.0, pltpu.roll(x, by, 1))
    high = jnp.where(lane >= 128 - by, 0.0, pltpu.roll(x, 128 - by, 1))
    return low + high


def row_above(x):
    return jnp.where(iota(0) == 0, 0.0, pltpu.roll(x, 1, 0))


def row_below(x):
    return jnp.where(iota(0) == 63, 0.0, pltpu.roll(x, 63, 0))


def fine_rate(buf, kn, p):
    centre = [[buf[p, sp, par] for par in range(2)] for sp in range(2)]
    kappa = [kn[p - 1, pl.ds(par, 64, stride=2), :] for par in range(2)]
    lap = []
    for sp in range(2):
        e, o = centre[sp]
        le = buf[p - 1, sp, 0] + buf[p + 1, sp, 0] + o + row_above(o) + beside_lanes(e, 1) - 6.0 * e
        lo = buf[p - 1, sp, 1] + buf[p + 1, sp, 1] + e + row_below(e) + beside_lanes(o, 1) - 6.0 * o
        lap.append((le, lo))
    out = [[None, None], [None, None]]
    for par in range(2):
        u, v = centre[0][par], centre[1][par]
        r = u * v * v
        out[0][par] = kappa[par] * lap[0][par] - r + FEED * (1.0 - u)
        out[1][par] = (0.5 * kappa[par]) * lap[1][par] + r - (FEED + KILL) * v
    return out


def each():
    return [(sp, par) for sp in range(2) for par in range(2)]


def pairs(su, sv):
    return jnp.where(even_lane(), su + pltpu.roll(su, 127, 1), sv + pltpu.roll(sv, 1, 1))


def restrict(buf, a, b):
    s = [buf[a, sp, 0] + buf[a, sp, 1] + buf[b, sp, 0] + buf[b, sp, 1] for sp in range(2)]
    return 0.125 * pairs(s[0], s[1])


def prolong(d):
    even = even_lane()
    return jnp.where(even, d, pltpu.roll(d, 1, 1)), jnp.where(even, pltpu.roll(d, 127, 1), d)


def local_rate(c):
    even = even_lane()
    u, v = prolong(c)
    r = u * v * v
    return jnp.where(even, -r, r) - jnp.where(even, FEED, FEED + KILL) * c


def coarse_lap(below, d, above):
    return below + above + row_above(d) + row_below(d) + beside_lanes(d, 2) - 6.0 * d


def kernel(
    n, init_ref, kap_ref, out_ref,
    nat, kn, x0, x1, x2, f0, g1, g2, g0, base, ex, v1p, v2p,
    d1c, b2c, kc, wi, wpk, d11c, b11c, dd, pd, td, d5, c5, c5own, a1p, e3,
    lsem, ssem, rsem,
):
    me = lax.axis_index("space")
    t = lax.axis_index("tm")
    c = lax.rem(me, 2)
    partner = me + 1 - 2 * c
    outer = me - 1 + 2 * c
    far_in = me + 2 - 4 * c
    far_out = me - 2 + 4 * c
    has_out = jnp.logical_and(outer >= 0, outer < n)
    has_far = jnp.logical_and(far_in >= 0, far_in < n)
    always = None
    first, second = t == 0, t == 1
    def across(other):
        row = jnp.logical_and(other // 2 != me // 2, other // 4 == me // 4)
        return jnp.where(row, 1 - t, t)

    t_out, t_fin, t_fout = across(outer), across(far_in), across(far_out)

    m_out = jnp.where(has_out, 1.0, 0.0).astype(F32)

    def when(cond, fn):
        if cond is None:
            fn()
        else:
            pl.when(cond)(fn)

    def both(a, b):
        if a is None:
            return b
        return a if b is None else jnp.logical_and(a, b)

    copies = []

    def copy(src, dst, tm, space, cond, back="same"):
        i = len(copies)
        cp = pltpu.make_async_remote_copy(
            src_ref=src, dst_ref=dst, send_sem=ssem.at[i], recv_sem=rsem.at[i],
            device_id=(tm, space), device_id_type=MESH)
        copies.append((cond, cp))
        return cond, cond if isinstance(back, str) else back, cp

    def start(*cs):
        for cond, _, cp in cs:
            when(cond, cp.start)

    def arrived(*cs):
        for _, back, cp in cs:
            when(back, cp.wait_recv)

    locals_ = [
        pltpu.make_async_copy(init_ref.at[:, 1 - c], nat.at[1], lsem.at[0]),
        pltpu.make_async_copy(init_ref.at[:, c], nat.at[2], lsem.at[1]),
        pltpu.make_async_copy(kap_ref.at[1 - c], kn.at[0], lsem.at[2]),
        pltpu.make_async_copy(kap_ref.at[c], kn.at[1], lsem.at[3]),
    ]
    for cp in locals_:
        cp.start()

    barrier = pltpu.get_barrier_semaphore()
    around = [(always, partner), (has_out, outer), (has_far, far_in), (has_out, far_out)]
    greet = [(t, cond, s) for cond, s in around] + [(1 - t, cond, s) for cond, s in [(always, me)] + around]
    for tm, cond, s in greet:
        when(cond, lambda tm=tm, s=s: pl.semaphore_signal(barrier, inc=1, device_id=(tm, s), device_id_type=MESH))

    @pl.when(jnp.logical_not(has_out))
    def _():
        zero_plane = jnp.zeros((2, 2, 64, 128), F32)
        for buf in (x1, x2):
            buf[4] = zero_plane
        nat[3] = jnp.zeros((2, 128, 128), F32)
        nat[4] = jnp.zeros((2, 128, 128), F32)
        kn[2] = jnp.zeros((128, 128), F32)
        zero = jnp.zeros((64, 128), F32)
        for buf in (d1c, d11c, c5):
            buf[3] = zero
            buf[4] = zero
        for buf in (b2c, kc, b11c, d5, a1p):
            buf[2] = zero
        e3[1] = zero

    @pl.when(jnp.logical_not(has_far))
    def _():
        zero = jnp.zeros((64, 128), F32)
        for buf in (d1c, d11c, c5):
            buf[0] = zero
        e3[0] = zero

    v2p[3] = jnp.zeros((2, 2, 64, 128), F32)
    pl.semaphore_wait(barrier, 3 + 4 * has_out.astype(jnp.int32) + 2 * has_far.astype(jnp.int32))

    for cp in locals_:
        cp.wait()
    p_init = copy(nat.at[1], nat.at[0], t, partner, always)
    o_init = copy(nat.at[2], nat.at[3], t_out, outer, has_out)
    o_kap = copy(kn.at[1], kn.at[2], t_out, outer, has_out)
    o_init2 = copy(nat.at[1], nat.at[4], t_out, outer, has_out)
    start(p_init, o_init, o_kap, o_init2)

    def convert(p):
        for sp, par in each():
            x0[p, sp, par] = nat[p, sp, pl.ds(par, 64, stride=2), :]

    convert(1)
    convert(2)
    ks = (kn[0, pl.ds(0, 64, stride=2), :] + kn[0, pl.ds(1, 64, stride=2), :]
          + kn[1, pl.ds(0, 64, stride=2), :] + kn[1, pl.ds(1, 64, stride=2), :])
    kc[1] = (0.125 * HALF / 4.0) * pairs(ks, 0.5 * ks)
    p_kc = copy(kc.at[1], kc.at[0], t, partner, always)
    o_kc = copy(kc.at[1], kc.at[2], t_out, outer, has_out)

    def masked(p):
        return jnp.where(p == 3, m_out, 1.0).astype(F32)

    def loop(lo, hi, body):
        def step(i, carry):
            body(i)
            return carry
        lax.fori_loop(lo, hi, step, 0)

    p_v1 = copy(x1.at[1], x1.at[0], t, partner, always)
    o_v1 = copy(x1.at[1], x1.at[4], t_out, outer, has_out)
    p_v2 = copy(x2.at[1], x2.at[0], t, partner, always)
    o_v2 = copy(x2.at[1], x2.at[4], t_out, outer, has_out)

    arrived(p_init)
    convert(0)

    def body_a1(p):
        @pl.when(p == 2)
        def _():
            arrived(o_init, o_kap, o_init2)
            convert(3)
            convert(4)

        f = fine_rate(x0, kn, p)
        m = masked(p)
        for sp, par in each():
            f0[p - 1, sp, par] = f[sp][par]
            x1[p, sp, par] = (x0[p, sp, par] + HALF * f[sp][par]) * m

        @pl.when(p == 1)
        def _():
            start(p_v1, o_v1, p_kc, o_kc)

    loop(1, 4, body_a1)

    def body_a2(p):
        @pl.when(p == 1)
        def _():
            arrived(p_v1)

        @pl.when(p == 3)
        def _():
            arrived(o_v1)

        g = fine_rate(x1, kn, p)
        m = masked(p)
        for sp, par in each():
            g1[p - 1, sp, par] = g[sp][par]
            x2[p, sp, par] = (x1[p, sp, par] + HALF * g[sp][par]) * m

        @pl.when(p == 1)
        def _():
            start(p_v2, o_v2)

    loop(1, 4, body_a2)

    def store_rate(dst, buf, p):
        g = fine_rate(buf, kn, p)
        for sp, par in each():
            dst[p - 1, sp, par] = g[sp][par]

    def body_a3(i):
        p = 2 - i

        @pl.when(p == 1)
        def _():
            arrived(p_v2)

        store_rate(g2, x2, p)

    loop(0, 2, body_a3)

    w0, w1, w2 = (restrict(x, 1, 2) for x in (x0, x1, x2))
    rf, r1, r2 = (restrict(x, 0, 1) for x in (f0, g1, g2))
    q0 = S0[0] * rf + S0[1] * r1 + S0[2] * r2
    q1 = S1[0] * rf + S1[1] * r1 + S1[2] * r2
    c1 = w0 + q0
    d1c[2] = c1 - w1
    b2c[1] = c1 + q1 + HALF * (local_rate(c1) - local_rate(w1))
    wpk[0] = w0
    wpk[1] = w2

    def spread(buf, at, cond, t_out=t, t_fin=t, t_fout=t):
        return [
            copy(buf.at[at], buf.at[3], t_out, outer, both(cond, has_out)),
            copy(buf.at[at], buf.at[4], t_fin, far_in, both(cond, has_far), both(cond, has_out)),
            copy(buf.at[at], buf.at[0], t_fout, far_out, both(cond, has_out), both(cond, has_far)),
            copy(buf.at[at], buf.at[1], t, partner, cond),
        ]

    def beside(buf, cond, t_out=t):
        return [
            copy(buf.at[1], buf.at[2], t_out, outer, both(cond, has_out)),
            copy(buf.at[1], buf.at[0], t, partner, cond),
        ]

    round2 = spread(d1c, 2, always, t_out, t_fin, t_fout) + beside(b2c, always, t_out) + [copy(wpk, wi, t, partner, always)]
    start(*round2)
    w0o = restrict(x0, 3, 4)
    arrived(p_kc, o_kc, o_v2)
    w2o = restrict(x2, 3, 4)
    store_rate(g2, x2, 3)

    def collect(p, start_at, f):
        for sp, par in each():
            a, b = g1[p - 1, sp, par], g2[p - 1, sp, par]
            base[p - 1, sp, par] = start_at[sp][par] + S0[0] * f[sp][par] + S0[1] * a + S0[2] * b
            ex[p - 1, sp, par] = S1[0] * f[sp][par] + (S1[1] - HALF) * a + S1[2] * b

    def fields(buf, p):
        return [[buf[p, sp, par] for par in range(2)] for sp in range(2)]

    def body_b1(p):
        collect(p, fields(x0, p), fields(f0, p - 1))

    loop(1, 4, body_b1)
    arrived(*round2)
    w0s = (wi[0], w0, w0o)
    w2s = (wi[1], w2, w2o)

    def corrected(d, b, j):
        r = b[j] + kc[j] * coarse_lap(d[j], d[j + 1], d[j + 2])
        return r * m_out if j == 2 else r

    c02 = [corrected(d1c, b2c, j) for j in range(3)]

    def correction(i, d):
        even = even_lane()
        for j in range(3):
            for sp, x in enumerate(prolong(d[j])):
                pd[i, j, sp] = x
                if j == 0:
                    continue
                low = jnp.where(iota(1) == 0, 0.0, pltpu.roll(x, 1, 1))
                high = jnp.where(iota(1) == 127, 0.0, pltpu.roll(x, 127, 1))
                t_ = jnp.where(even, low, high) - 3.0 * x
                td[i, j - 1, sp, 0] = t_ + row_above(x)
                td[i, j - 1, sp, 1] = t_ + row_below(x)

    def corrected_rate(i, src, p):
        own, across = p // 3 + 1, (2 * p - 2) % 3
        pu, pv = pd[i, own, 0], pd[i, own, 1]
        au, av = pd[i, across, 0], pd[i, across, 1]
        out = [[None, None], [None, None]]
        for par in range(2):
            k = kn[p - 1, pl.ds(par, 64, stride=2), :]
            u, v = src[p, 0, par], src[p, 1, par]
            un, vn = u + pu, v + pv
            r = un * vn * vn - u * v * v
            out[0][par] = k * (td[i, own - 1, 0, par] + au) - r - FEED * pu
            out[1][par] = (0.5 * k) * (td[i, own - 1, 1, par] + av) + r - (FEED + KILL) * pv
        return out

    @pl.when(first)
    def _():
        correction(0, [d1c[j + 1] for j in range(3)])
        correction(1, [c02[j] - w2s[j] for j in range(3)])

    r3 = spread(d11c, 2, second) + beside(b11c, second)

    @pl.when(second)
    def _():
        d10 = [c02[j] - w0s[j] for j in range(3)]
        c11 = c02[1] + q0 + kc[1] * coarse_lap(*d10) + HALF * (local_rate(c02[1]) - local_rate(w0))
        d11c[2] = c11 - w1
        b11c[1] = c11 + q1 + HALF * (local_rate(c11) - local_rate(w1))

    start(*r3)

    @pl.when(second)
    def _():
        correction(0, [c02[j] - w0s[j] for j in range(3)])
        correction(1, [c02[j] - w2s[j] for j in range(3)])

        def body(p):
            df = corrected_rate(0, x0, p)
            dr = corrected_rate(1, x2, p)
            own = p // 3 + 1
            y, f = fields(x2, p), fields(f0, p - 1)
            for sp, par in each():
                r = g2[p - 1, sp, par] + dr[sp][par]
                f[sp][par] = f[sp][par] + df[sp][par]
                g0[p - 1, sp, par] = r
                y[sp][par] = y[sp][par] + pd[1, own, sp] + HALF * (r - f[sp][par])
            collect(p, y, f)
        loop(1, 4, body)
        dd[0] = restrict(g0, 0, 1)

    @pl.when(first)
    def _():
        dd[0] = rf

    arrived(*r3)

    @pl.when(second)
    def _():
        correction(0, [d11c[j + 1] for j in range(3)])
        correction(1, [corrected(d11c, b11c, j) - w2s[j] for j in range(3)])

    p_v1p = copy(v1p.at[1], v1p.at[0], t, partner, always)
    p_v2p = copy(v2p.at[1], v2p.at[0], t, partner, always)
    r_e = [copy(e3.at[2], e3.at[1], t, outer, has_out), copy(e3.at[2], e3.at[0], t, far_out, has_out, has_far)]

    def body_c1(p):
        fa = corrected_rate(0, x1, p)
        fb = corrected_rate(1, x2, p)
        m = masked(p)
        for sp, par in each():
            a, b = fa[sp][par], fb[sp][par]
            v1p[p, sp, par] = (base[p - 1, sp, par] + S0[1] * a + S0[2] * b) * m
            ex[p - 1, sp, par] = ex[p - 1, sp, par] + (S1[1] - HALF) * a + S1[2] * b

        @pl.when(p == 1)
        def _():
            start(p_v1p)

    loop(1, 4, body_c1)

    def body_c2(i):
        p = 2 - i

        @pl.when(p == 1)
        def _():
            arrived(p_v1p)

        g = fine_rate(v1p, kn, p)
        for sp, par in each():
            g1[p - 1, sp, par] = g[sp][par]
            v2p[p, sp, par] = v1p[p, sp, par] + ex[p - 1, sp, par] + HALF * g[sp][par]

        @pl.when(p == 2)
        def _():
            k = [kn[2, pl.ds(par, 64, stride=2), :] for par in range(2)]
            su = k[0] * v2p[2, 0, 0] + k[1] * v2p[2, 0, 1]
            sv = k[0] * v2p[2, 1, 0] + k[1] * v2p[2, 1, 1]
            e3[2] = 0.125 * pairs(su, 0.5 * sv)
            start(*r_e)

        @pl.when(p == 1)
        def _():
            start(p_v2p)

    loop(0, 2, body_c2)

    def body_c3(i):
        p = 2 - i

        @pl.when(p == 1)
        def _():
            arrived(p_v2p)

        store_rate(g2, v2p, p)

    loop(0, 2, body_c3)

    w1, w2 = restrict(v1p, 1, 2), restrict(v2p, 1, 2)
    rf, r1, r2 = dd[0], restrict(g1, 0, 1), restrict(g2, 0, 1)
    q0 = S0[0] * rf + S0[1] * r1 + S0[2] * r2
    q1 = S1[0] * rf + S1[1] * r1 + S1[2] * r2

    r5 = beside(d5, first)
    r6 = [copy(c5own.at[0], c5.at[at], 1, s, both(first, cond), both(second, back))
          for at, cond, back, s in ((3, has_out, has_out, outer), (4, has_far, has_out, far_in),
                                    (0, has_out, has_far, far_out), (2, always, always, me),
                                    (1, always, always, partner))]
    r7 = beside(a1p, second)

    @pl.when(first)
    def _():
        d5[1] = w0 + q0 - w1
        start(*r5)

    @pl.when(second)
    def _():
        a1p[1] = q0 - HALF * local_rate(c02[1]) - w1
        start(*r7)

    arrived(*r_e)
    e_own = (S0[2] * e3[0], S0[2] * e3[1], S0[2] * e3[2])
    q0 = q0 + e_own[1]
    q1 = q1 + S1[2] * e3[1]

    @pl.when(first)
    def _():
        c1 = w0 + q0
        b = c1 + q1 + HALF * (local_rate(c1) - local_rate(w1))
        arrived(*r5)
        end = b + kc[1] * coarse_lap(d5[0] + e_own[0], c1 - w1, d5[2] + e_own[2])
        c5own[0] = end - c02[1]
        start(*r6)
        dd[1] = end - w2

    arrived(*r7)

    arrived(*r6)

    @pl.when(second)
    def _():
        d11, c11 = [], None
        for j in range(3):
            c10 = c5[j + 1] + c02[j]
            r = c10 + (a1p[j] + e_own[j]) + kc[j] * coarse_lap(c5[j], c5[j + 1], c5[j + 2]) + HALF * local_rate(c10)
            if j == 1:
                c11 = r + w1
            d11.append(r * m_out if j == 2 else r)
        end = c11 + q1 + kc[1] * coarse_lap(*d11) + HALF * (local_rate(c11) - local_rate(w1))
        dd[1] = end - w2

    up = prolong(dd[1])
    for p, plane in ((1, 1 - c), (2, c)):
        for sp, par in each():
            out_ref[0, sp, plane, pl.ds(par, 64, stride=2), :] = v2p[p, sp, par] + up[sp]

    for cond, cp in copies:
        when(cond, cp.wait_send)


def shards(n, initial, kappa):
    fine = lambda k: pltpu.VMEM((k, 2, 2, 64, 128), F32)
    coarse = lambda k: pltpu.VMEM((k, 64, 128), F32)
    return pl.pallas_call(
        functools.partial(kernel, n),
        out_shape=pltpu.VMEM((1,) + initial.shape, F32),
        in_specs=[pl.BlockSpec(memory_space=pltpu.HBM)] * 2,
        out_specs=pl.BlockSpec(memory_space=pltpu.VMEM),
        scratch_shapes=[
            pltpu.VMEM((5, 2, 128, 128), F32), pltpu.VMEM((3, 128, 128), F32),
            fine(5), fine(5), fine(5), fine(3), fine(3), fine(3), fine(3), fine(3), fine(3), fine(4), fine(4),
            coarse(5), coarse(3), coarse(3), coarse(2), coarse(2), coarse(5), coarse(3), coarse(2),
            pltpu.VMEM((2, 3, 2, 64, 128), F32), pltpu.VMEM((2, 2, 2, 2, 64, 128), F32),
            coarse(3), coarse(5), coarse(1), coarse(3), coarse(3),
            pltpu.SemaphoreType.DMA((4,)), pltpu.SemaphoreType.DMA((N_COPIES,)), pltpu.SemaphoreType.DMA((N_COPIES,)),
        ],
        compiler_params=pltpu.CompilerParams(
            collective_id=0, has_side_effects=True, vmem_limit_bytes=63 * 1024 * 1024),
    )(initial, kappa)


def solution(mesh):
    return jax.shard_map(
        functools.partial(shards, mesh.shape["space"]),
        mesh=mesh,
        in_specs=(P(None, "space", None, None), P("space", None, None)),
        out_specs=P("tm", None, "space", None, None),
        check_vma=False,
    )
```

```python
import functools

import jax
import jax.numpy as jnp
from jax import lax
from jax.experimental import pallas as pl
from jax.experimental.pallas import tpu as pltpu
from jax.sharding import PartitionSpec as P

MESH = pl.DeviceIdType.MESH
F32 = jnp.float32
STEP = 0.25
HALF = 0.125
FEED = 0.04
KILL = 0.06
S0 = (STEP * 5.0 / 24.0, STEP / 3.0, -STEP / 24.0)
S1 = (-STEP / 24.0, STEP / 3.0, STEP * 5.0 / 24.0)
N_COPIES = 48


def iota(dim):
    return lax.broadcasted_iota(jnp.int32, (64, 128), dim)


def even_lane():
    return iota(1) % 2 == 0


def beside_lanes(x, by):
    lane = iota(1)
    low = jnp.where(lane < by, 0.0, pltpu.roll(x, by, 1))
    high = jnp.where(lane >= 128 - by, 0.0, pltpu.roll(x, 128 - by, 1))
    return low + high


def row_above(x):
    return jnp.where(iota(0) == 0, 0.0, pltpu.roll(x, 1, 0))


def row_below(x):
    return jnp.where(iota(0) == 63, 0.0, pltpu.roll(x, 63, 0))


def kappas(kn, p):
    return [kn[p, pl.ds(par, 64, stride=2), :] for par in range(2)]


def fine_rate(buf, kn, p, below=True, above=True):
    centre = [[buf[p, sp, par] for par in range(2)] for sp in range(2)]
    kappa = kappas(kn, p)
    lap = []
    for sp in range(2):
        e, o = centre[sp]
        le = o + row_above(o) + beside_lanes(e, 1) - 6.0 * e
        lo = e + row_below(e) + beside_lanes(o, 1) - 6.0 * o
        for there, q in ((below, p - 1), (above, p + 1)):
            if there:
                le, lo = le + buf[q, sp, 0], lo + buf[q, sp, 1]
        lap.append((le, lo))
    out = [[None, None], [None, None]]
    for par in range(2):
        u, v = centre[0][par], centre[1][par]
        r = u * v * v
        out[0][par] = kappa[par] * lap[0][par] - r + FEED * (1.0 - u)
        out[1][par] = (0.5 * kappa[par]) * lap[1][par] + r - (FEED + KILL) * v
    return out


def across(buf, q, kn, p):
    return [[(k if sp == 0 else 0.5 * k) * buf[q, sp, par] for par, k in enumerate(kappas(kn, p))] for sp in range(2)]


def each():
    return [(sp, par) for sp in range(2) for par in range(2)]


def pairs(su, sv):
    return jnp.where(even_lane(), su + pltpu.roll(su, 127, 1), sv + pltpu.roll(sv, 1, 1))


def restrict(buf, a, b):
    s = [buf[a, sp, 0] + buf[a, sp, 1] + buf[b, sp, 0] + buf[b, sp, 1] for sp in range(2)]
    return 0.125 * pairs(s[0], s[1])


def restrict_plane(g):
    return 0.125 * pairs(g[0][0] + g[0][1], g[1][0] + g[1][1])


def prolong(d):
    even = even_lane()
    return jnp.where(even, d, pltpu.roll(d, 1, 1)), jnp.where(even, pltpu.roll(d, 127, 1), d)


def local_rate(c):
    even = even_lane()
    u, v = prolong(c)
    r = u * v * v
    return jnp.where(even, -r, r) - jnp.where(even, FEED, FEED + KILL) * c


def coarse_lap(below, d, above):
    return below + above + row_above(d) + row_below(d) + beside_lanes(d, 2) - 6.0 * d


def kernel(
    n, init_ref, kap_ref, out_ref,
    nat, kn, x0, x1, x2, f0, g1, g2, g0, base, ex, v1p, v2p,
    d1c, b2c, kc, wi, wpk, d11c, b11c, dd, pd, td, d5, c5, c5own, a1p, e3,
    lsem, ssem, rsem,
):
    me = lax.axis_index("space")
    t = lax.axis_index("tm")
    c = lax.rem(me, 2)
    partner = me + 1 - 2 * c
    outer = me - 1 + 2 * c
    far_in = me + 2 - 4 * c
    far_out = me - 2 + 4 * c
    has_out = jnp.logical_and(outer >= 0, outer < n)
    has_far = jnp.logical_and(far_in >= 0, far_in < n)
    always = None
    first, second = t == 0, t == 1
    def other_tm(other):
        row = jnp.logical_and(other // 2 != me // 2, other // 4 == me // 4)
        return jnp.where(row, 1 - t, t)

    t_out, t_fin, t_fout = other_tm(outer), other_tm(far_in), other_tm(far_out)

    m_out = jnp.where(has_out, 1.0, 0.0).astype(F32)

    def when(cond, fn):
        if cond is None:
            fn()
        else:
            pl.when(cond)(fn)

    def both(a, b):
        if a is None:
            return b
        return a if b is None else jnp.logical_and(a, b)

    copies = []

    def copy(src, dst, tm, space, cond, back="same"):
        i = len(copies)
        cp = pltpu.make_async_remote_copy(
            src_ref=src, dst_ref=dst, send_sem=ssem.at[i], recv_sem=rsem.at[i],
            device_id=(tm, space), device_id_type=MESH)
        copies.append((cond, cp))
        return cond, cond if isinstance(back, str) else back, cp

    def start(*cs):
        for cond, _, cp in cs:
            when(cond, cp.start)

    def arrived(*cs):
        for _, back, cp in cs:
            when(back, cp.wait_recv)

    locals_ = [
        pltpu.make_async_copy(init_ref.at[:, 1 - c], nat.at[1], lsem.at[0]),
        pltpu.make_async_copy(init_ref.at[:, c], nat.at[2], lsem.at[1]),
        pltpu.make_async_copy(kap_ref.at[1 - c], kn.at[1], lsem.at[2]),
        pltpu.make_async_copy(kap_ref.at[c], kn.at[2], lsem.at[3]),
    ]
    for cp in locals_:
        cp.start()

    barrier = pltpu.get_barrier_semaphore()
    around = [(always, partner), (has_out, outer), (has_far, far_in), (has_out, far_out)]
    greet = [(t, cond, s) for cond, s in around] + [(1 - t, cond, s) for cond, s in [(always, me)] + around]
    for tm, cond, s in greet:
        when(cond, lambda tm=tm, s=s: pl.semaphore_signal(barrier, inc=1, device_id=(tm, s), device_id_type=MESH))

    @pl.when(jnp.logical_not(has_out))
    def _():
        zero_plane = jnp.zeros((2, 2, 64, 128), F32)
        for buf in (x1, x2):
            buf[4] = zero_plane
        nat[3] = jnp.zeros((2, 128, 128), F32)
        nat[4] = jnp.zeros((2, 128, 128), F32)
        kn[3] = jnp.zeros((128, 128), F32)
        zero = jnp.zeros((64, 128), F32)
        for buf in (d1c, d11c, c5):
            buf[3] = zero
            buf[4] = zero
        for buf in (b2c, kc, b11c, d5, a1p):
            buf[2] = zero
        e3[1] = zero

    @pl.when(jnp.logical_not(has_far))
    def _():
        zero = jnp.zeros((64, 128), F32)
        for buf in (d1c, d11c, c5):
            buf[0] = zero
        e3[0] = zero

    pl.semaphore_wait(barrier, 3 + 4 * has_out.astype(jnp.int32) + 2 * has_far.astype(jnp.int32))

    for cp in locals_:
        cp.wait()
    p_init = copy(nat.at[1], nat.at[0], t, partner, always)
    o_init = copy(nat.at[2], nat.at[3], t_out, outer, has_out)
    p_kap = copy(kn.at[1], kn.at[0], t, partner, always)
    o_kap = copy(kn.at[2], kn.at[3], t_out, outer, has_out)
    o_init2 = copy(nat.at[1], nat.at[4], t_out, outer, has_out)
    start(p_init, o_init, o_kap, o_init2, p_kap)

    def convert(p):
        for sp, par in each():
            x0[p, sp, par] = nat[p, sp, pl.ds(par, 64, stride=2), :]

    convert(1)
    convert(2)
    ks = sum(kappas(kn, 1) + kappas(kn, 2))
    kc[1] = (0.125 * HALF / 4.0) * pairs(ks, 0.5 * ks)
    p_kc = copy(kc.at[1], kc.at[0], t, partner, always)
    o_kc = copy(kc.at[1], kc.at[2], t_out, outer, has_out)

    def masked(p):
        return jnp.where(p == 3, m_out, 1.0).astype(F32)

    def loop(lo, hi, body):
        def step(i, carry):
            body(i)
            return carry
        lax.fori_loop(lo, hi, step, 0)

    p_v1 = copy(x1.at[1], x1.at[0], t, partner, always)
    o_v1 = copy(x1.at[1], x1.at[4], t_out, outer, has_out)
    p_v2 = copy(x2.at[1], x2.at[0], t, partner, always)
    o_v2 = copy(x2.at[1], x2.at[4], t_out, outer, has_out)

    arrived(p_init)
    convert(0)

    def body_a1(p):
        @pl.when(p == 2)
        def _():
            arrived(o_init, o_kap, o_init2)
            convert(3)
            convert(4)

        f = fine_rate(x0, kn, p)
        m = masked(p)
        for sp, par in each():
            f0[p - 1, sp, par] = f[sp][par]
            x1[p, sp, par] = (x0[p, sp, par] + HALF * f[sp][par]) * m

        @pl.when(p == 1)
        def _():
            start(p_v1, o_v1)

    loop(1, 4, body_a1)

    def body_a2(p):
        @pl.when(p == 1)
        def _():
            arrived(p_v1)

        g = fine_rate(x1, kn, p)
        for sp, par in each():
            g1[p - 1, sp, par] = g[sp][par]
            x2[p, sp, par] = x1[p, sp, par] + HALF * g[sp][par]

        @pl.when(p == 1)
        def _():
            start(p_v2, p_kc, o_kc)

    loop(1, 3, body_a2)

    def store(dst, p, g):
        for sp, par in each():
            dst[p - 1, sp, par] = g[sp][par]

    store(g1, 3, fine_rate(x1, kn, 3, above=False))
    store(g2, 2, fine_rate(x2, kn, 2, above=False))
    w0, w1, w2 = (restrict(x, 1, 2) for x in (x0, x1, x2))
    rf, r1 = restrict(f0, 0, 1), restrict(g1, 0, 1)
    arrived(p_v2)
    store(g2, 1, fine_rate(x2, kn, 1))
    r2 = restrict(g2, 0, 1)
    q0 = S0[0] * rf + S0[1] * r1 + S0[2] * r2
    q1 = S1[0] * rf + S1[1] * r1 + S1[2] * r2

    arrived(o_v1)
    more = across(x1, 4, kn, 3)
    for sp, par in each():
        r = g1[2, sp, par] + more[sp][par]
        g1[2, sp, par] = r
        x2[3, sp, par] = (x1[3, sp, par] + HALF * r) * m_out
    more = across(x2, 3, kn, 2)
    for sp, par in each():
        g2[1, sp, par] = g2[1, sp, par] + more[sp][par]
    r2 = restrict_plane(more)
    q0 = q0 + S0[2] * r2
    q1 = q1 + S1[2] * r2
    c1 = w0 + q0
    d1c[2] = c1 - w1
    b2c[1] = c1 + q1 + HALF * (local_rate(c1) - local_rate(w1))
    wpk[0] = w0
    wpk[1] = w2

    def spread(buf, at, cond, t_out=t, t_fin=t, t_fout=t):
        return [
            copy(buf.at[at], buf.at[3], t_out, outer, both(cond, has_out)),
            copy(buf.at[at], buf.at[4], t_fin, far_in, both(cond, has_far), both(cond, has_out)),
            copy(buf.at[at], buf.at[0], t_fout, far_out, both(cond, has_out), both(cond, has_far)),
            copy(buf.at[at], buf.at[1], t, partner, cond),
        ]

    def beside(buf, cond, t_out=t):
        return [
            copy(buf.at[1], buf.at[2], t_out, outer, both(cond, has_out)),
            copy(buf.at[1], buf.at[0], t, partner, cond),
        ]

    round2 = spread(d1c, 2, always, t_out, t_fin, t_fout) + beside(b2c, always, t_out) + [copy(wpk, wi, t, partner, always)]
    start(*round2)
    start(o_v2)
    w0o = restrict(x0, 3, 4)
    arrived(p_kc, o_kc)

    def collect(p, start_at, f):
        for sp, par in each():
            a, b = g1[p - 1, sp, par], g2[p - 1, sp, par]
            base[p, sp, par] = start_at[sp][par] + S0[0] * f[sp][par] + S0[1] * a + S0[2] * b
            ex[p, sp, par] = S1[0] * f[sp][par] + (S1[1] - HALF) * a + S1[2] * b

    def fields(buf, p):
        return [[buf[p, sp, par] for par in range(2)] for sp in range(2)]

    def body_b1(p):
        collect(p, fields(x0, p), fields(f0, p - 1))

    loop(1, 3, body_b1)
    p_base = copy(base.at[1], base.at[0], t, partner, always)

    @pl.when(first)
    def _():
        start(p_base)

    arrived(*round2)
    w0s = (wi[0], w0, w0o)

    def corrected(d, b, j):
        r = b[j] + kc[j] * coarse_lap(d[j], d[j + 1], d[j + 2])
        return r * m_out if j == 2 else r

    c02 = [corrected(d1c, b2c, j) for j in range(3)]

    def correction(i, d):
        even = even_lane()
        for j in range(3):
            for sp, x in enumerate(prolong(d[j])):
                pd[i, j, sp] = x
                low = jnp.where(iota(1) == 0, 0.0, pltpu.roll(x, 1, 1))
                high = jnp.where(iota(1) == 127, 0.0, pltpu.roll(x, 127, 1))
                t_ = jnp.where(even, low, high) - 3.0 * x
                td[i, j, sp, 0] = t_ + row_above(x)
                td[i, j, sp, 1] = t_ + row_below(x)

    def corrected_rate(i, src, p):
        own = (p + 1) // 2
        beyond = own + 1 - 2 * (p % 2)
        pu, pv = pd[i, own, 0], pd[i, own, 1]
        au, av = pd[i, beyond, 0], pd[i, beyond, 1]
        out = [[None, None], [None, None]]
        for par in range(2):
            k = kappas(kn, p)[par]
            u, v = src[p, 0, par], src[p, 1, par]
            un, vn = u + pu, v + pv
            r = un * vn * vn - u * v * v
            out[0][par] = k * (td[i, own, 0, par] + au) - r - FEED * pu
            out[1][par] = (0.5 * k) * (td[i, own, 1, par] + av) + r - (FEED + KILL) * pv
        return out

    r3 = spread(d11c, 2, second) + beside(b11c, second)

    @pl.when(second)
    def _():
        d10 = [c02[j] - w0s[j] for j in range(3)]
        c11 = c02[1] + q0 + kc[1] * coarse_lap(*d10) + HALF * (local_rate(c02[1]) - local_rate(w0))
        d11c[2] = c11 - w1
        b11c[1] = c11 + q1 + HALF * (local_rate(c11) - local_rate(w1))

    start(*r3)

    arrived(o_v2)
    w2s = (wi[1], w2, restrict(x2, 3, 4))
    store(g2, 3, fine_rate(x2, kn, 3))

    @pl.when(first)
    def _():
        body_b1(3)
        correction(0, [d1c[j + 1] for j in range(3)])
        correction(1, [c02[j] - w2s[j] for j in range(3)])

    @pl.when(second)
    def _():
        correction(0, [c02[j] - w0s[j] for j in range(3)])
        correction(1, [c02[j] - w2s[j] for j in range(3)])

        def body(p):
            df = corrected_rate(0, x0, p)
            dr = corrected_rate(1, x2, p)
            own = (p + 1) // 2
            y, f = fields(x2, p), fields(f0, p - 1)
            for sp, par in each():
                r = g2[p - 1, sp, par] + dr[sp][par]
                f[sp][par] = f[sp][par] + df[sp][par]
                g0[p - 1, sp, par] = r
                y[sp][par] = y[sp][par] + pd[1, own, sp] + HALF * (r - f[sp][par])
            collect(p, y, f)
        loop(1, 4, body)
        start(p_base)
        dd[0] = restrict(g0, 0, 1)

    @pl.when(first)
    def _():
        dd[0] = rf

    arrived(*r3)

    @pl.when(second)
    def _():
        correction(0, [d11c[j + 1] for j in range(3)])
        correction(1, [corrected(d11c, b11c, j) - w2s[j] for j in range(3)])

    p_v2p = copy(v2p.at[1], v2p.at[0], t, partner, always)
    r_e = [copy(e3.at[2], e3.at[1], t, outer, has_out), copy(e3.at[2], e3.at[0], t, far_out, has_out, has_far)]

    def second_node(p):
        g = fine_rate(v1p, kn, p)
        for sp, par in each():
            g1[p - 1, sp, par] = g[sp][par]
            v2p[p, sp, par] = v1p[p, sp, par] + ex[p, sp, par] + HALF * g[sp][par]

    arrived(p_base, p_kap)

    def body_c1(p):
        fa = corrected_rate(0, x1, p)
        fb = corrected_rate(1, x2, p)
        m = masked(p)
        for sp, par in each():
            a, b = fa[sp][par], fb[sp][par]
            v1p[p, sp, par] = (base[p, sp, par] + S0[1] * a + S0[2] * b) * m
            ex[p, sp, par] = ex[p, sp, par] + (S1[1] - HALF) * a + S1[2] * b

        @pl.when(p == 2)
        def _():
            second_node(1)
            start(p_v2p)

    loop(0, 4, body_c1)
    second_node(2)
    e3[2] = restrict_plane(across(v2p, 2, kn, 3))
    start(*r_e)
    store(g2, 2, fine_rate(v2p, kn, 2, above=False))
    store(g2, 1, fine_rate(v2p, kn, 1, below=False))

    w1, w2 = restrict(v1p, 1, 2), restrict(v2p, 1, 2)
    rf, r1, r2 = dd[0], restrict(g1, 0, 1), restrict(g2, 0, 1)
    q0 = S0[0] * rf + S0[1] * r1 + S0[2] * r2
    q1 = S1[0] * rf + S1[1] * r1 + S1[2] * r2
    arrived(p_v2p)
    r2 = restrict_plane(across(v2p, 0, kn, 1))
    q0 = q0 + S0[2] * r2
    q1 = q1 + S1[2] * r2

    r5 = beside(d5, first)
    r6 = [copy(c5own.at[0], c5.at[at], 1, s, both(first, cond), both(second, back))
          for at, cond, back, s in ((3, has_out, has_out, outer), (4, has_far, has_out, far_in),
                                    (0, has_out, has_far, far_out), (2, always, always, me),
                                    (1, always, always, partner))]
    r7 = beside(a1p, second)

    @pl.when(first)
    def _():
        d5[1] = w0 + q0 - w1
        start(*r5)

    @pl.when(second)
    def _():
        a1p[1] = q0 - HALF * local_rate(c02[1]) - w1
        start(*r7)

    arrived(*r_e)
    e_own = (S0[2] * e3[0], S0[2] * e3[1], S0[2] * e3[2])
    q0 = q0 + e_own[1]
    q1 = q1 + S1[2] * e3[1]

    @pl.when(first)
    def _():
        c1 = w0 + q0
        b = c1 + q1 + HALF * (local_rate(c1) - local_rate(w1))
        arrived(*r5)
        end = b + kc[1] * coarse_lap(d5[0] + e_own[0], c1 - w1, d5[2] + e_own[2])
        c5own[0] = end - c02[1]
        start(*r6)
        dd[1] = end - w2

    arrived(*r7)

    arrived(*r6)

    @pl.when(second)
    def _():
        d11, c11 = [], None
        for j in range(3):
            c10 = c5[j + 1] + c02[j]
            r = c10 + (a1p[j] + e_own[j]) + kc[j] * coarse_lap(c5[j], c5[j + 1], c5[j + 2]) + HALF * local_rate(c10)
            if j == 1:
                c11 = r + w1
            d11.append(r * m_out if j == 2 else r)
        end = c11 + q1 + kc[1] * coarse_lap(*d11) + HALF * (local_rate(c11) - local_rate(w1))
        dd[1] = end - w2

    up = prolong(dd[1])
    for p, plane in ((1, 1 - c), (2, c)):
        for sp, par in each():
            out_ref[0, sp, plane, pl.ds(par, 64, stride=2), :] = v2p[p, sp, par] + up[sp]

    for cond, cp in copies:
        when(cond, cp.wait_send)


def shards(n, initial, kappa):
    fine = lambda k: pltpu.VMEM((k, 2, 2, 64, 128), F32)
    coarse = lambda k: pltpu.VMEM((k, 64, 128), F32)
    return pl.pallas_call(
        functools.partial(kernel, n),
        out_shape=pltpu.VMEM((1,) + initial.shape, F32),
        in_specs=[pl.BlockSpec(memory_space=pltpu.HBM)] * 2,
        out_specs=pl.BlockSpec(memory_space=pltpu.VMEM),
        scratch_shapes=[
            pltpu.VMEM((5, 2, 128, 128), F32), pltpu.VMEM((4, 128, 128), F32),
            fine(5), fine(5), fine(5), fine(3), fine(3), fine(3), fine(3), fine(4), fine(4), fine(4), fine(3),
            coarse(5), coarse(3), coarse(3), coarse(2), coarse(2), coarse(5), coarse(3), coarse(2),
            pltpu.VMEM((2, 3, 2, 64, 128), F32), pltpu.VMEM((2, 3, 2, 2, 64, 128), F32),
            coarse(3), coarse(5), coarse(1), coarse(3), coarse(3),
            pltpu.SemaphoreType.DMA((4,)), pltpu.SemaphoreType.DMA((N_COPIES,)), pltpu.SemaphoreType.DMA((N_COPIES,)),
        ],
        compiler_params=pltpu.CompilerParams(
            collective_id=0, has_side_effects=True, vmem_limit_bytes=63 * 1024 * 1024),
    )(initial, kappa)


def solution(mesh):
    return jax.shard_map(
        functools.partial(shards, mesh.shape["space"]),
        mesh=mesh,
        in_specs=(P(None, "space", None, None), P("space", None, None)),
        out_specs=P("tm", None, "space", None, None),
        check_vma=False,
    )
```

```python
import functools

import jax
import jax.numpy as jnp
from jax import lax
from jax.experimental import pallas as pl
from jax.experimental.pallas import tpu as pltpu
from jax.sharding import PartitionSpec as P

MESH = pl.DeviceIdType.MESH
F32 = jnp.float32
STEP = 0.25
HALF = 0.125
FEED = 0.04
KILL = 0.06
S0 = (STEP * 5.0 / 24.0, STEP / 3.0, -STEP / 24.0)
S1 = (-STEP / 24.0, STEP / 3.0, STEP * 5.0 / 24.0)
N_COPIES = 48


def iota(dim):
    return lax.broadcasted_iota(jnp.int32, (64, 128), dim)


def even_lane():
    return iota(1) % 2 == 0


def beside_lanes(x, by):
    lane = iota(1)
    low = jnp.where(lane < by, 0.0, pltpu.roll(x, by, 1))
    high = jnp.where(lane >= 128 - by, 0.0, pltpu.roll(x, 128 - by, 1))
    return low + high


def row_above(x):
    return jnp.where(iota(0) == 0, 0.0, pltpu.roll(x, 1, 0))


def row_below(x):
    return jnp.where(iota(0) == 63, 0.0, pltpu.roll(x, 63, 0))


def kappas(kn, p):
    return [kn[p, pl.ds(par, 64, stride=2), :] for par in range(2)]


def fine_rate(buf, kn, p, below=True, above=True):
    centre = [[buf[p, sp, par] for par in range(2)] for sp in range(2)]
    kappa = kappas(kn, p)
    lap = []
    for sp in range(2):
        e, o = centre[sp]
        le = o + row_above(o) + beside_lanes(e, 1) - 6.0 * e
        lo = e + row_below(e) + beside_lanes(o, 1) - 6.0 * o
        for there, q in ((below, p - 1), (above, p + 1)):
            if there:
                le, lo = le + buf[q, sp, 0], lo + buf[q, sp, 1]
        lap.append((le, lo))
    out = [[None, None], [None, None]]
    for par in range(2):
        u, v = centre[0][par], centre[1][par]
        r = u * v * v
        out[0][par] = kappa[par] * lap[0][par] - r + FEED * (1.0 - u)
        out[1][par] = (0.5 * kappa[par]) * lap[1][par] + r - (FEED + KILL) * v
    return out


def across(buf, q, kn, p):
    return [[(k if sp == 0 else 0.5 * k) * buf[q, sp, par] for par, k in enumerate(kappas(kn, p))] for sp in range(2)]


def each():
    return [(sp, par) for sp in range(2) for par in range(2)]


def pairs(su, sv):
    return jnp.where(even_lane(), su + pltpu.roll(su, 127, 1), sv + pltpu.roll(sv, 1, 1))


def restrict(buf, a, b):
    s = [buf[a, sp, 0] + buf[a, sp, 1] + buf[b, sp, 0] + buf[b, sp, 1] for sp in range(2)]
    return 0.125 * pairs(s[0], s[1])


def restrict_plane(g):
    return 0.125 * pairs(g[0][0] + g[0][1], g[1][0] + g[1][1])


def prolong(d):
    even = even_lane()
    return jnp.where(even, d, pltpu.roll(d, 1, 1)), jnp.where(even, pltpu.roll(d, 127, 1), d)


def local_rate(c):
    even = even_lane()
    u, v = prolong(c)
    r = u * v * v
    return jnp.where(even, -r, r) - jnp.where(even, FEED, FEED + KILL) * c


def coarse_lap(below, d, above):
    return below + above + row_above(d) + row_below(d) + beside_lanes(d, 2) - 6.0 * d


def kernel(
    n, init_ref, kap_ref, out_ref,
    nat, kn, x0, x1, x2, f0, g1, g2, g0, base, ex, v1p, v2p,
    d1c, b2c, kc, wi, wpk, d11c, b11c, dd, pd, td, d5, c5, c5own, a1p, e3,
    lsem, ssem, rsem,
):
    me = lax.axis_index("space")
    t = lax.axis_index("tm")
    c = lax.rem(me, 2)
    partner = me + 1 - 2 * c
    outer = me - 1 + 2 * c
    far_in = me + 2 - 4 * c
    far_out = me - 2 + 4 * c
    has_out = jnp.logical_and(outer >= 0, outer < n)
    has_far = jnp.logical_and(far_in >= 0, far_in < n)
    always = None
    first, second = t == 0, t == 1
    def other_tm(other):
        row = jnp.logical_and(other // 2 != me // 2, other // 4 == me // 4)
        return jnp.where(row, 1 - t, t)

    t_out, t_fin, t_fout = other_tm(outer), other_tm(far_in), other_tm(far_out)

    m_out = jnp.where(has_out, 1.0, 0.0).astype(F32)

    def when(cond, fn):
        if cond is None:
            fn()
        else:
            pl.when(cond)(fn)

    def both(a, b):
        if a is None:
            return b
        return a if b is None else jnp.logical_and(a, b)

    copies = []

    def copy(src, dst, tm, space, cond, back="same"):
        i = len(copies)
        cp = pltpu.make_async_remote_copy(
            src_ref=src, dst_ref=dst, send_sem=ssem.at[i], recv_sem=rsem.at[i],
            device_id=(tm, space), device_id_type=MESH)
        copies.append((cond, cp))
        return cond, cond if isinstance(back, str) else back, cp

    def start(*cs):
        for cond, _, cp in cs:
            when(cond, cp.start)

    def arrived(*cs):
        for _, back, cp in cs:
            when(back, cp.wait_recv)

    locals_ = [
        pltpu.make_async_copy(init_ref.at[:, 1 - c], nat.at[1], lsem.at[0]),
        pltpu.make_async_copy(init_ref.at[:, c], nat.at[2], lsem.at[1]),
        pltpu.make_async_copy(kap_ref.at[1 - c], kn.at[1], lsem.at[2]),
        pltpu.make_async_copy(kap_ref.at[c], kn.at[2], lsem.at[3]),
    ]
    for cp in locals_:
        cp.start()

    barrier = pltpu.get_barrier_semaphore()
    around = [(always, partner), (has_out, outer), (has_far, far_in), (has_out, far_out)]
    greet = [(t, cond, s) for cond, s in around] + [(1 - t, cond, s) for cond, s in [(always, me)] + around]
    for tm, cond, s in greet:
        when(cond, lambda tm=tm, s=s: pl.semaphore_signal(barrier, inc=1, device_id=(tm, s), device_id_type=MESH))

    @pl.when(jnp.logical_not(has_out))
    def _():
        zero_plane = jnp.zeros((2, 2, 64, 128), F32)
        for buf in (x1, x2):
            buf[4] = zero_plane
        nat[3] = jnp.zeros((2, 128, 128), F32)
        nat[4] = jnp.zeros((2, 128, 128), F32)
        kn[3] = jnp.zeros((128, 128), F32)
        zero = jnp.zeros((64, 128), F32)
        for buf in (d1c, d11c, c5):
            buf[3] = zero
            buf[4] = zero
        for buf in (b2c, kc, b11c, d5, a1p):
            buf[2] = zero
        e3[1] = zero

    @pl.when(jnp.logical_not(has_far))
    def _():
        zero = jnp.zeros((64, 128), F32)
        for buf in (d1c, d11c, c5):
            buf[0] = zero
        e3[0] = zero

    pl.semaphore_wait(barrier, 3 + 4 * has_out.astype(jnp.int32) + 2 * has_far.astype(jnp.int32))

    for cp in locals_:
        cp.wait()
    p_init = copy(nat.at[1], nat.at[0], t, partner, always)
    o_init = copy(nat.at[2], nat.at[3], t_out, outer, has_out)
    p_kap = copy(kn.at[1], kn.at[0], t, partner, always)
    o_kap = copy(kn.at[2], kn.at[3], t_out, outer, has_out)
    o_init2 = copy(nat.at[1], nat.at[4], t_out, outer, has_out)
    start(p_init, o_init, o_kap, o_init2, p_kap)

    def convert(p):
        for sp, par in each():
            x0[p, sp, par] = nat[p, sp, pl.ds(par, 64, stride=2), :]

    convert(1)
    convert(2)
    ks = sum(kappas(kn, 1) + kappas(kn, 2))
    kc[1] = (0.125 * HALF / 4.0) * pairs(ks, 0.5 * ks)
    p_kc = copy(kc.at[1], kc.at[0], t, partner, always)
    o_kc = copy(kc.at[1], kc.at[2], t_out, outer, has_out)

    def masked(p):
        return jnp.where(p == 3, m_out, 1.0).astype(F32)

    def loop(lo, hi, body):
        def step(i, carry):
            body(i)
            return carry
        lax.fori_loop(lo, hi, step, 0)

    p_v1 = copy(x1.at[1], x1.at[0], t, partner, always)
    o_v1 = copy(x1.at[1], x1.at[4], t_out, outer, has_out)
    p_v2 = copy(x2.at[1], x2.at[0], t, partner, always)
    o_v2 = copy(x2.at[1], x2.at[4], t_out, outer, has_out)

    arrived(p_init)
    convert(0)

    def body_a1(p):
        @pl.when(p == 2)
        def _():
            arrived(o_init, o_kap, o_init2)
            convert(3)
            convert(4)

        f = fine_rate(x0, kn, p)
        m = masked(p)
        for sp, par in each():
            f0[p - 1, sp, par] = f[sp][par]
            x1[p, sp, par] = (x0[p, sp, par] + HALF * f[sp][par]) * m

        @pl.when(p == 1)
        def _():
            start(p_v1, o_v1)

    loop(1, 4, body_a1)

    def body_a2(p):
        @pl.when(p == 1)
        def _():
            arrived(p_v1)

        g = fine_rate(x1, kn, p)
        for sp, par in each():
            g1[p - 1, sp, par] = g[sp][par]
            x2[p, sp, par] = x1[p, sp, par] + HALF * g[sp][par]

        @pl.when(p == 1)
        def _():
            start(p_v2, p_kc, o_kc)

    loop(1, 3, body_a2)

    def store(dst, p, g):
        for sp, par in each():
            dst[p - 1, sp, par] = g[sp][par]

    store(g1, 3, fine_rate(x1, kn, 3, above=False))
    store(g2, 2, fine_rate(x2, kn, 2, above=False))
    w0, w1, w2 = (restrict(x, 1, 2) for x in (x0, x1, x2))
    rf, r1 = restrict(f0, 0, 1), restrict(g1, 0, 1)
    arrived(p_v2)
    store(g2, 1, fine_rate(x2, kn, 1))
    r2 = restrict(g2, 0, 1)
    q0 = S0[0] * rf + S0[1] * r1 + S0[2] * r2
    q1 = S1[0] * rf + S1[1] * r1 + S1[2] * r2

    arrived(o_v1)
    more = across(x1, 4, kn, 3)
    for sp, par in each():
        r = g1[2, sp, par] + more[sp][par]
        g1[2, sp, par] = r
        x2[3, sp, par] = (x1[3, sp, par] + HALF * r) * m_out
    more = across(x2, 3, kn, 2)
    for sp, par in each():
        g2[1, sp, par] = g2[1, sp, par] + more[sp][par]
    r2 = restrict_plane(more)
    q0 = q0 + S0[2] * r2
    q1 = q1 + S1[2] * r2
    c1 = w0 + q0
    d1c[2] = c1 - w1
    b2c[1] = c1 + q1 + HALF * (local_rate(c1) - local_rate(w1))
    wpk[0] = w0
    wpk[1] = w2

    def spread(buf, at, cond, t_out=t, t_fin=t, t_fout=t):
        return [
            copy(buf.at[at], buf.at[0], t_fout, far_out, both(cond, has_out), both(cond, has_far)),
            copy(buf.at[at], buf.at[4], t_fin, far_in, both(cond, has_far), both(cond, has_out)),
            copy(buf.at[at], buf.at[3], t_out, outer, both(cond, has_out)),
            copy(buf.at[at], buf.at[1], t, partner, cond),
        ]

    def beside(buf, cond, t_out=t):
        return [
            copy(buf.at[1], buf.at[2], t_out, outer, both(cond, has_out)),
            copy(buf.at[1], buf.at[0], t, partner, cond),
        ]

    round2 = spread(d1c, 2, always, t_out, t_fin, t_fout) + beside(b2c, always, t_out) + [copy(wpk, wi, t, partner, always)]
    start(*round2)
    start(o_v2)
    w0o = restrict(x0, 3, 4)
    arrived(p_kc, o_kc)

    def collect(p, start_at, f):
        for sp, par in each():
            a, b = g1[p - 1, sp, par], g2[p - 1, sp, par]
            base[p, sp, par] = start_at[sp][par] + S0[0] * f[sp][par] + S0[1] * a + S0[2] * b
            ex[p, sp, par] = S1[0] * f[sp][par] + (S1[1] - HALF) * a + S1[2] * b

    def fields(buf, p):
        return [[buf[p, sp, par] for par in range(2)] for sp in range(2)]

    def body_b1(p):
        collect(p, fields(x0, p), fields(f0, p - 1))

    loop(1, 3, body_b1)
    p_base = copy(base.at[1], base.at[0], t, partner, always)

    @pl.when(first)
    def _():
        start(p_base)

    arrived(*round2)
    w0s = (wi[0], w0, w0o)

    def corrected(d, b, j):
        r = b[j] + kc[j] * coarse_lap(d[j], d[j + 1], d[j + 2])
        return r * m_out if j == 2 else r

    c02 = [corrected(d1c, b2c, j) for j in range(3)]

    def correction(i, d):
        even = even_lane()
        lane = iota(1)
        for j in range(3):
            back, on, back2, on2 = (pltpu.roll(d[j], by, 1) for by in (1, 127, 2, 126))
            species = (
                (jnp.where(even, d[j], back), jnp.where(even, back2, on)),
                (jnp.where(even, on, d[j]), jnp.where(even, back, on2)),
            )
            for sp, (x, beside_x) in enumerate(species):
                pd[i, j, sp] = x
                t_ = jnp.where((lane == 0) | (lane == 127), 0.0, beside_x) - 3.0 * x
                td[i, j, sp, 0] = t_ + row_above(x)
                td[i, j, sp, 1] = t_ + row_below(x)

    def corrected_rate(i, src, p):
        own = (p + 1) // 2
        beyond = own + 1 - 2 * (p % 2)
        pu, pv = pd[i, own, 0], pd[i, own, 1]
        au, av = pd[i, beyond, 0], pd[i, beyond, 1]
        out = [[None, None], [None, None]]
        for par in range(2):
            k = kappas(kn, p)[par]
            u, v = src[p, 0, par], src[p, 1, par]
            un, vn = u + pu, v + pv
            r = un * vn * vn - u * v * v
            out[0][par] = k * (td[i, own, 0, par] + au) - r - FEED * pu
            out[1][par] = (0.5 * k) * (td[i, own, 1, par] + av) + r - (FEED + KILL) * pv
        return out

    r3 = spread(d11c, 2, second) + beside(b11c, second)

    @pl.when(second)
    def _():
        d10 = [c02[j] - w0s[j] for j in range(3)]
        c11 = c02[1] + q0 + kc[1] * coarse_lap(*d10) + HALF * (local_rate(c02[1]) - local_rate(w0))
        d11c[2] = c11 - w1
        b11c[1] = c11 + q1 + HALF * (local_rate(c11) - local_rate(w1))

    start(*r3)

    arrived(o_v2)
    w2s = (wi[1], w2, restrict(x2, 3, 4))
    store(g2, 3, fine_rate(x2, kn, 3))

    @pl.when(first)
    def _():
        body_b1(3)
        correction(0, [d1c[j + 1] for j in range(3)])
        correction(1, [c02[j] - w2s[j] for j in range(3)])

    @pl.when(second)
    def _():
        correction(0, [c02[j] - w0s[j] for j in range(3)])
        correction(1, [c02[j] - w2s[j] for j in range(3)])

        def body(p):
            df = corrected_rate(0, x0, p)
            dr = corrected_rate(1, x2, p)
            own = (p + 1) // 2
            y, f = fields(x2, p), fields(f0, p - 1)
            for sp, par in each():
                r = g2[p - 1, sp, par] + dr[sp][par]
                f[sp][par] = f[sp][par] + df[sp][par]
                g0[p - 1, sp, par] = r
                y[sp][par] = y[sp][par] + pd[1, own, sp] + HALF * (r - f[sp][par])
            collect(p, y, f)
        loop(1, 4, body)
        start(p_base)
        dd[0] = restrict(g0, 0, 1)

    @pl.when(first)
    def _():
        dd[0] = rf

    arrived(*r3)

    @pl.when(second)
    def _():
        correction(0, [d11c[j + 1] for j in range(3)])
        correction(1, [corrected(d11c, b11c, j) - w2s[j] for j in range(3)])

    p_v2p = copy(v2p.at[1], v2p.at[0], t, partner, always)
    r_e = [copy(e3.at[2], e3.at[1], t, outer, has_out), copy(e3.at[2], e3.at[0], t, far_out, has_out, has_far)]

    def second_node(p):
        g = fine_rate(v1p, kn, p)
        for sp, par in each():
            g1[p - 1, sp, par] = g[sp][par]
            v2p[p, sp, par] = v1p[p, sp, par] + ex[p, sp, par] + HALF * g[sp][par]

    arrived(p_base, p_kap)

    def body_c1(p):
        fa = corrected_rate(0, x1, p)
        fb = corrected_rate(1, x2, p)
        m = masked(p)
        for sp, par in each():
            a, b = fa[sp][par], fb[sp][par]
            v1p[p, sp, par] = (base[p, sp, par] + S0[1] * a + S0[2] * b) * m
            ex[p, sp, par] = ex[p, sp, par] + (S1[1] - HALF) * a + S1[2] * b

        @pl.when(p == 2)
        def _():
            second_node(1)
            start(p_v2p)

    loop(0, 4, body_c1)
    second_node(2)
    e3[2] = restrict_plane(across(v2p, 2, kn, 3))
    start(*r_e)
    store(g2, 2, fine_rate(v2p, kn, 2, above=False))
    store(g2, 1, fine_rate(v2p, kn, 1, below=False))

    w1, w2 = restrict(v1p, 1, 2), restrict(v2p, 1, 2)
    rf, r1, r2 = dd[0], restrict(g1, 0, 1), restrict(g2, 0, 1)
    q0 = S0[0] * rf + S0[1] * r1 + S0[2] * r2
    q1 = S1[0] * rf + S1[1] * r1 + S1[2] * r2
    arrived(p_v2p)
    r2 = restrict_plane(across(v2p, 0, kn, 1))
    q0 = q0 + S0[2] * r2
    q1 = q1 + S1[2] * r2

    r5 = beside(d5, first)
    r6 = [copy(c5own.at[0], c5.at[at], 1, s, both(first, cond), both(second, back))
          for at, cond, back, s in ((3, has_out, has_out, outer), (4, has_far, has_out, far_in),
                                    (0, has_out, has_far, far_out), (2, always, always, me),
                                    (1, always, always, partner))]
    r7 = beside(a1p, second)

    @pl.when(first)
    def _():
        d5[1] = w0 + q0 - w1
        start(*r5)

    @pl.when(second)
    def _():
        a1p[1] = q0 - HALF * local_rate(c02[1]) - w1
        start(*r7)

    arrived(*r_e)
    e_own = (S0[2] * e3[0], S0[2] * e3[1], S0[2] * e3[2])
    q0 = q0 + e_own[1]
    q1 = q1 + S1[2] * e3[1]

    @pl.when(first)
    def _():
        c1 = w0 + q0
        b = c1 + q1 + HALF * (local_rate(c1) - local_rate(w1))
        arrived(*r5)
        end = b + kc[1] * coarse_lap(d5[0] + e_own[0], c1 - w1, d5[2] + e_own[2])
        c5own[0] = end - c02[1]
        start(*r6)
        dd[1] = end - w2

    arrived(*r7)

    arrived(*r6)

    @pl.when(second)
    def _():
        d11, c11 = [], None
        for j in range(3):
            c10 = c5[j + 1] + c02[j]
            r = c10 + (a1p[j] + e_own[j]) + kc[j] * coarse_lap(c5[j], c5[j + 1], c5[j + 2]) + HALF * local_rate(c10)
            if j == 1:
                c11 = r + w1
            d11.append(r * m_out if j == 2 else r)
        end = c11 + q1 + kc[1] * coarse_lap(*d11) + HALF * (local_rate(c11) - local_rate(w1))
        dd[1] = end - w2

    up = prolong(dd[1])
    for p, plane in ((1, 1 - c), (2, c)):
        for sp, par in each():
            out_ref[0, sp, plane, pl.ds(par, 64, stride=2), :] = v2p[p, sp, par] + up[sp]

    for cond, cp in copies:
        when(cond, cp.wait_send)


def shards(n, initial, kappa):
    fine = lambda k: pltpu.VMEM((k, 2, 2, 64, 128), F32)
    coarse = lambda k: pltpu.VMEM((k, 64, 128), F32)
    return pl.pallas_call(
        functools.partial(kernel, n),
        out_shape=pltpu.VMEM((1,) + initial.shape, F32),
        in_specs=[pl.BlockSpec(memory_space=pltpu.HBM)] * 2,
        out_specs=pl.BlockSpec(memory_space=pltpu.VMEM),
        scratch_shapes=[
            pltpu.VMEM((5, 2, 128, 128), F32), pltpu.VMEM((4, 128, 128), F32),
            fine(5), fine(5), fine(5), fine(3), fine(3), fine(3), fine(3), fine(4), fine(4), fine(4), fine(3),
            coarse(5), coarse(3), coarse(3), coarse(2), coarse(2), coarse(5), coarse(3), coarse(2),
            pltpu.VMEM((2, 3, 2, 64, 128), F32), pltpu.VMEM((2, 3, 2, 2, 64, 128), F32),
            coarse(3), coarse(5), coarse(1), coarse(3), coarse(3),
            pltpu.SemaphoreType.DMA((4,)), pltpu.SemaphoreType.DMA((N_COPIES,)), pltpu.SemaphoreType.DMA((N_COPIES,)),
        ],
        compiler_params=pltpu.CompilerParams(
            collective_id=0, has_side_effects=True, vmem_limit_bytes=63 * 1024 * 1024),
    )(initial, kappa)


def solution(mesh):
    return jax.shard_map(
        functools.partial(shards, mesh.shape["space"]),
        mesh=mesh,
        in_specs=(P(None, "space", None, None), P("space", None, None)),
        out_specs=P("tm", None, "space", None, None),
        check_vma=False,
    )
```

```python
import functools

import jax
import jax.numpy as jnp
from jax import lax
from jax.experimental import pallas as pl
from jax.experimental.pallas import tpu as pltpu
from jax.sharding import PartitionSpec as P

MESH = pl.DeviceIdType.MESH
F32 = jnp.float32
STEP = 0.25
HALF = 0.125
FEED = 0.04
KILL = 0.06
S0 = (STEP * 5.0 / 24.0, STEP / 3.0, -STEP / 24.0)
S1 = (-STEP / 24.0, STEP / 3.0, STEP * 5.0 / 24.0)
N_COPIES = 48


def iota(dim):
    return lax.broadcasted_iota(jnp.int32, (64, 128), dim)


def even_lane():
    return iota(1) % 2 == 0


def beside_lanes(x, by):
    lane = iota(1)
    low = jnp.where(lane < by, 0.0, pltpu.roll(x, by, 1))
    high = jnp.where(lane >= 128 - by, 0.0, pltpu.roll(x, 128 - by, 1))
    return low + high


def row_above(x):
    return jnp.where(iota(0) == 0, 0.0, pltpu.roll(x, 1, 0))


def row_below(x):
    return jnp.where(iota(0) == 63, 0.0, pltpu.roll(x, 63, 0))


def kappas(kn, p):
    return [kn[p, pl.ds(par, 64, stride=2), :] for par in range(2)]


def fine_rate(buf, kn, p, below=True, above=True):
    centre = [[buf[p, sp, par] for par in range(2)] for sp in range(2)]
    kappa = kappas(kn, p)
    lap = []
    for sp in range(2):
        e, o = centre[sp]
        le = o + row_above(o) + beside_lanes(e, 1) - 6.0 * e
        lo = e + row_below(e) + beside_lanes(o, 1) - 6.0 * o
        for there, q in ((below, p - 1), (above, p + 1)):
            if there:
                le, lo = le + buf[q, sp, 0], lo + buf[q, sp, 1]
        lap.append((le, lo))
    out = [[None, None], [None, None]]
    for par in range(2):
        u, v = centre[0][par], centre[1][par]
        r = u * v * v
        out[0][par] = kappa[par] * lap[0][par] - r + FEED * (1.0 - u)
        out[1][par] = (0.5 * kappa[par]) * lap[1][par] + r - (FEED + KILL) * v
    return out


def across(buf, q, kn, p):
    return [[(k if sp == 0 else 0.5 * k) * buf[q, sp, par] for par, k in enumerate(kappas(kn, p))] for sp in range(2)]


def each():
    return [(sp, par) for sp in range(2) for par in range(2)]


def pairs(su, sv):
    return jnp.where(even_lane(), su + pltpu.roll(su, 127, 1), sv + pltpu.roll(sv, 1, 1))


def restrict(buf, a, b):
    s = [buf[a, sp, 0] + buf[a, sp, 1] + buf[b, sp, 0] + buf[b, sp, 1] for sp in range(2)]
    return 0.125 * pairs(s[0], s[1])


def restrict_plane(g):
    return 0.125 * pairs(g[0][0] + g[0][1], g[1][0] + g[1][1])


def prolong(d):
    even = even_lane()
    return jnp.where(even, d, pltpu.roll(d, 1, 1)), jnp.where(even, pltpu.roll(d, 127, 1), d)


def local_rate(c):
    even = even_lane()
    u, v = prolong(c)
    r = u * v * v
    return jnp.where(even, -r, r) - jnp.where(even, FEED, FEED + KILL) * c


def coarse_lap(below, d, above):
    return below + above + row_above(d) + row_below(d) + beside_lanes(d, 2) - 6.0 * d


def kernel(
    n, init_ref, kap_ref, out_ref,
    nat, kn, x0, x1, x2, f0, g1, g2, g0, base, ex, v1p, v2p,
    d1c, b2c, kc, wi, wpk, d11c, b11c, dd, pd, td, d5, c5, c5own, a1p, e3,
    lsem, ssem, rsem,
):
    me = lax.axis_index("space")
    t = lax.axis_index("tm")
    c = lax.rem(me, 2)
    partner = me + 1 - 2 * c
    outer = me - 1 + 2 * c
    far_in = me + 2 - 4 * c
    far_out = me - 2 + 4 * c
    has_out = jnp.logical_and(outer >= 0, outer < n)
    has_far = jnp.logical_and(far_in >= 0, far_in < n)
    always = None
    first, second = t == 0, t == 1
    def other_tm(other, rows, z, y):
        chip = other // 2 != me // 2
        row = jnp.logical_and(chip, other // 4 == me // 4)
        step_y = other // 16 != me // 16
        step_z = jnp.logical_and(other // 4 != me // 4, jnp.logical_not(step_y))
        turn = (other // 2) % 2 != (me // 2) % 2
        swap = jnp.zeros((), jnp.bool_)
        for wanted, there in ((rows, row), (z, jnp.logical_and(step_z, turn)), (y, step_y)):
            if wanted:
                swap = jnp.logical_or(swap, there)
        return jnp.where(swap, 1 - t, t)

    t_out, t_fin, t_fout = (other_tm(s, True, False, False) for s in (outer, far_in, far_out))
    t_inputs, t_late = other_tm(outer, True, True, False), other_tm(outer, True, False, True)

    m_out = jnp.where(has_out, 1.0, 0.0).astype(F32)

    def when(cond, fn):
        if cond is None:
            fn()
        else:
            pl.when(cond)(fn)

    def both(a, b):
        if a is None:
            return b
        return a if b is None else jnp.logical_and(a, b)

    copies = []

    def copy(src, dst, tm, space, cond, back="same"):
        i = len(copies)
        cp = pltpu.make_async_remote_copy(
            src_ref=src, dst_ref=dst, send_sem=ssem.at[i], recv_sem=rsem.at[i],
            device_id=(tm, space), device_id_type=MESH)
        copies.append((cond, cp))
        return cond, cond if isinstance(back, str) else back, cp

    def start(*cs):
        for cond, _, cp in cs:
            when(cond, cp.start)

    def arrived(*cs):
        for _, back, cp in cs:
            when(back, cp.wait_recv)

    locals_ = [
        pltpu.make_async_copy(init_ref.at[:, 1 - c], nat.at[1], lsem.at[0]),
        pltpu.make_async_copy(init_ref.at[:, c], nat.at[2], lsem.at[1]),
        pltpu.make_async_copy(kap_ref.at[1 - c], kn.at[1], lsem.at[2]),
        pltpu.make_async_copy(kap_ref.at[c], kn.at[2], lsem.at[3]),
    ]
    for cp in locals_:
        cp.start()

    barrier = pltpu.get_barrier_semaphore()
    around = [(always, partner), (has_out, outer), (has_far, far_in), (has_out, far_out)]
    greet = [(t, cond, s) for cond, s in around] + [(1 - t, cond, s) for cond, s in [(always, me)] + around]
    for tm, cond, s in greet:
        when(cond, lambda tm=tm, s=s: pl.semaphore_signal(barrier, inc=1, device_id=(tm, s), device_id_type=MESH))

    @pl.when(jnp.logical_not(has_out))
    def _():
        zero_plane = jnp.zeros((2, 2, 64, 128), F32)
        for buf in (x1, x2):
            buf[4] = zero_plane
        nat[3] = jnp.zeros((2, 128, 128), F32)
        nat[4] = jnp.zeros((2, 128, 128), F32)
        kn[3] = jnp.zeros((128, 128), F32)
        zero = jnp.zeros((64, 128), F32)
        for buf in (d1c, d11c, c5):
            buf[3] = zero
            buf[4] = zero
        for buf in (b2c, kc, b11c, d5, a1p):
            buf[2] = zero
        e3[1] = zero

    @pl.when(jnp.logical_not(has_far))
    def _():
        zero = jnp.zeros((64, 128), F32)
        for buf in (d1c, d11c, c5):
            buf[0] = zero
        e3[0] = zero

    pl.semaphore_wait(barrier, 3 + 4 * has_out.astype(jnp.int32) + 2 * has_far.astype(jnp.int32))

    for cp in locals_:
        cp.wait()
    p_init = copy(nat.at[1], nat.at[0], t, partner, always)
    o_init = copy(nat.at[2], nat.at[3], t_inputs, outer, has_out)
    p_kap = copy(kn.at[1], kn.at[0], t, partner, always)
    o_kap = copy(kn.at[2], kn.at[3], t_inputs, outer, has_out)
    o_init2 = copy(nat.at[1], nat.at[4], t_inputs, outer, has_out)
    start(p_init, o_init, o_kap, o_init2, p_kap)

    def convert(p):
        for sp, par in each():
            x0[p, sp, par] = nat[p, sp, pl.ds(par, 64, stride=2), :]

    convert(1)
    convert(2)
    ks = sum(kappas(kn, 1) + kappas(kn, 2))
    kc[1] = (0.125 * HALF / 4.0) * pairs(ks, 0.5 * ks)
    p_kc = copy(kc.at[1], kc.at[0], t, partner, always)
    o_kc = copy(kc.at[1], kc.at[2], t_late, outer, has_out)

    def masked(p):
        return jnp.where(p == 3, m_out, 1.0).astype(F32)

    def loop(lo, hi, body):
        def step(i, carry):
            body(i)
            return carry
        lax.fori_loop(lo, hi, step, 0)

    p_v1 = copy(x1.at[1], x1.at[0], t, partner, always)
    o_v1 = copy(x1.at[1], x1.at[4], t_out, outer, has_out)
    p_v2 = copy(x2.at[1], x2.at[0], t, partner, always)
    o_v2 = copy(x2.at[1], x2.at[4], t_late, outer, has_out)

    arrived(p_init)
    convert(0)

    def body_a1(p):
        @pl.when(p == 2)
        def _():
            arrived(o_init, o_kap, o_init2)
            convert(3)
            convert(4)

        f = fine_rate(x0, kn, p)
        m = masked(p)
        for sp, par in each():
            f0[p - 1, sp, par] = f[sp][par]
            x1[p, sp, par] = (x0[p, sp, par] + HALF * f[sp][par]) * m

        @pl.when(p == 1)
        def _():
            start(p_v1, o_v1)

    loop(1, 4, body_a1)

    def body_a2(p):
        @pl.when(p == 1)
        def _():
            arrived(p_v1)

        g = fine_rate(x1, kn, p)
        for sp, par in each():
            g1[p - 1, sp, par] = g[sp][par]
            x2[p, sp, par] = x1[p, sp, par] + HALF * g[sp][par]

        @pl.when(p == 1)
        def _():
            start(p_v2, p_kc, o_kc)

    loop(1, 3, body_a2)

    def store(dst, p, g):
        for sp, par in each():
            dst[p - 1, sp, par] = g[sp][par]

    store(g1, 3, fine_rate(x1, kn, 3, above=False))
    store(g2, 2, fine_rate(x2, kn, 2, above=False))
    w0, w1, w2 = (restrict(x, 1, 2) for x in (x0, x1, x2))
    rf, r1 = restrict(f0, 0, 1), restrict(g1, 0, 1)
    arrived(p_v2)
    store(g2, 1, fine_rate(x2, kn, 1))
    r2 = restrict(g2, 0, 1)
    q0 = S0[0] * rf + S0[1] * r1 + S0[2] * r2
    q1 = S1[0] * rf + S1[1] * r1 + S1[2] * r2

    arrived(o_v1)
    more = across(x1, 4, kn, 3)
    for sp, par in each():
        r = g1[2, sp, par] + more[sp][par]
        g1[2, sp, par] = r
        x2[3, sp, par] = (x1[3, sp, par] + HALF * r) * m_out
    more = across(x2, 3, kn, 2)
    for sp, par in each():
        g2[1, sp, par] = g2[1, sp, par] + more[sp][par]
    r2 = restrict_plane(more)
    q0 = q0 + S0[2] * r2
    q1 = q1 + S1[2] * r2
    c1 = w0 + q0
    d1c[2] = c1 - w1
    b2c[1] = c1 + q1 + HALF * (local_rate(c1) - local_rate(w1))
    wpk[0] = w0
    wpk[1] = w2

    def spread(buf, at, cond, t_out=t, t_fin=t, t_fout=t):
        return [
            copy(buf.at[at], buf.at[0], t_fout, far_out, both(cond, has_out), both(cond, has_far)),
            copy(buf.at[at], buf.at[4], t_fin, far_in, both(cond, has_far), both(cond, has_out)),
            copy(buf.at[at], buf.at[3], t_out, outer, both(cond, has_out)),
            copy(buf.at[at], buf.at[1], t, partner, cond),
        ]

    def beside(buf, cond, t_out=t):
        return [
            copy(buf.at[1], buf.at[2], t_out, outer, both(cond, has_out)),
            copy(buf.at[1], buf.at[0], t, partner, cond),
        ]

    round2 = spread(d1c, 2, always, t_out, t_fin, t_fout) + beside(b2c, always, t_out) + [copy(wpk, wi, t, partner, always)]
    start(*round2)
    start(o_v2)
    w0o = restrict(x0, 3, 4)
    arrived(p_kc, o_kc)

    def collect(p, start_at, f):
        for sp, par in each():
            a, b = g1[p - 1, sp, par], g2[p - 1, sp, par]
            base[p, sp, par] = start_at[sp][par] + S0[0] * f[sp][par] + S0[1] * a + S0[2] * b
            ex[p, sp, par] = S1[0] * f[sp][par] + (S1[1] - HALF) * a + S1[2] * b

    def fields(buf, p):
        return [[buf[p, sp, par] for par in range(2)] for sp in range(2)]

    def body_b1(p):
        collect(p, fields(x0, p), fields(f0, p - 1))

    loop(1, 3, body_b1)
    p_base = copy(base.at[1], base.at[0], t, partner, always)

    @pl.when(first)
    def _():
        start(p_base)

    arrived(*round2)
    w0s = (wi[0], w0, w0o)

    def corrected(d, b, j):
        r = b[j] + kc[j] * coarse_lap(d[j], d[j + 1], d[j + 2])
        return r * m_out if j == 2 else r

    c02 = [corrected(d1c, b2c, j) for j in range(3)]

    def correction(i, d):
        even = even_lane()
        lane = iota(1)
        for j in range(3):
            back, on, back2, on2 = (pltpu.roll(d[j], by, 1) for by in (1, 127, 2, 126))
            species = (
                (jnp.where(even, d[j], back), jnp.where(even, back2, on)),
                (jnp.where(even, on, d[j]), jnp.where(even, back, on2)),
            )
            for sp, (x, beside_x) in enumerate(species):
                pd[i, j, sp] = x
                t_ = jnp.where((lane == 0) | (lane == 127), 0.0, beside_x) - 3.0 * x
                td[i, j, sp, 0] = t_ + row_above(x)
                td[i, j, sp, 1] = t_ + row_below(x)

    def corrected_rate(i, src, p):
        own = (p + 1) // 2
        beyond = own + 1 - 2 * (p % 2)
        pu, pv = pd[i, own, 0], pd[i, own, 1]
        au, av = pd[i, beyond, 0], pd[i, beyond, 1]
        out = [[None, None], [None, None]]
        for par in range(2):
            k = kappas(kn, p)[par]
            u, v = src[p, 0, par], src[p, 1, par]
            un, vn = u + pu, v + pv
            r = un * vn * vn - u * v * v
            out[0][par] = k * (td[i, own, 0, par] + au) - r - FEED * pu
            out[1][par] = (0.5 * k) * (td[i, own, 1, par] + av) + r - (FEED + KILL) * pv
        return out

    r3 = spread(d11c, 2, second) + beside(b11c, second)

    @pl.when(second)
    def _():
        d10 = [c02[j] - w0s[j] for j in range(3)]
        c11 = c02[1] + q0 + kc[1] * coarse_lap(*d10) + HALF * (local_rate(c02[1]) - local_rate(w0))
        d11c[2] = c11 - w1
        b11c[1] = c11 + q1 + HALF * (local_rate(c11) - local_rate(w1))

    start(*r3)

    arrived(o_v2)
    w2s = (wi[1], w2, restrict(x2, 3, 4))
    store(g2, 3, fine_rate(x2, kn, 3))

    @pl.when(first)
    def _():
        body_b1(3)
        correction(0, [d1c[j + 1] for j in range(3)])
        correction(1, [c02[j] - w2s[j] for j in range(3)])

    @pl.when(second)
    def _():
        correction(0, [c02[j] - w0s[j] for j in range(3)])
        correction(1, [c02[j] - w2s[j] for j in range(3)])

        def body(p):
            df = corrected_rate(0, x0, p)
            dr = corrected_rate(1, x2, p)
            own = (p + 1) // 2
            y, f = fields(x2, p), fields(f0, p - 1)
            for sp, par in each():
                r = g2[p - 1, sp, par] + dr[sp][par]
                f[sp][par] = f[sp][par] + df[sp][par]
                g0[p - 1, sp, par] = r
                y[sp][par] = y[sp][par] + pd[1, own, sp] + HALF * (r - f[sp][par])
            collect(p, y, f)
        loop(1, 4, body)
        start(p_base)
        dd[0] = restrict(g0, 0, 1)

    @pl.when(first)
    def _():
        dd[0] = rf

    arrived(*r3)

    @pl.when(second)
    def _():
        correction(0, [d11c[j + 1] for j in range(3)])
        correction(1, [corrected(d11c, b11c, j) - w2s[j] for j in range(3)])

    p_v2p = copy(v2p.at[1], v2p.at[0], t, partner, always)
    r_e = [copy(e3.at[2], e3.at[0], t, far_out, has_out, has_far), copy(e3.at[2], e3.at[1], t, outer, has_out)]

    def second_node(p):
        g = fine_rate(v1p, kn, p)
        for sp, par in each():
            g1[p - 1, sp, par] = g[sp][par]
            v2p[p, sp, par] = v1p[p, sp, par] + ex[p, sp, par] + HALF * g[sp][par]

    arrived(p_base, p_kap)

    def body_c1(p):
        fa = corrected_rate(0, x1, p)
        fb = corrected_rate(1, x2, p)
        m = masked(p)
        for sp, par in each():
            a, b = fa[sp][par], fb[sp][par]
            v1p[p, sp, par] = (base[p, sp, par] + S0[1] * a + S0[2] * b) * m
            ex[p, sp, par] = ex[p, sp, par] + (S1[1] - HALF) * a + S1[2] * b

        @pl.when(p == 2)
        def _():
            second_node(1)
            start(p_v2p)

    loop(0, 4, body_c1)
    second_node(2)
    e3[2] = restrict_plane(across(v2p, 2, kn, 3))
    start(*r_e)
    store(g2, 2, fine_rate(v2p, kn, 2, above=False))
    store(g2, 1, fine_rate(v2p, kn, 1, below=False))

    w1, w2 = restrict(v1p, 1, 2), restrict(v2p, 1, 2)
    rf, r1, r2 = dd[0], restrict(g1, 0, 1), restrict(g2, 0, 1)
    q0 = S0[0] * rf + S0[1] * r1 + S0[2] * r2
    q1 = S1[0] * rf + S1[1] * r1 + S1[2] * r2
    arrived(p_v2p)
    r2 = restrict_plane(across(v2p, 0, kn, 1))
    q0 = q0 + S0[2] * r2
    q1 = q1 + S1[2] * r2

    r5 = beside(d5, first)
    r6 = [copy(c5own.at[0], c5.at[at], 1, s, both(first, cond), both(second, back))
          for at, cond, back, s in ((3, has_out, has_out, outer), (4, has_far, has_out, far_in),
                                    (0, has_out, has_far, far_out), (2, always, always, me),
                                    (1, always, always, partner))]
    r7 = beside(a1p, second)

    @pl.when(first)
    def _():
        d5[1] = w0 + q0 - w1
        start(*r5)

    @pl.when(second)
    def _():
        a1p[1] = q0 - HALF * local_rate(c02[1]) - w1
        start(*r7)

    arrived(*r_e)
    e_own = (S0[2] * e3[0], S0[2] * e3[1], S0[2] * e3[2])
    q0 = q0 + e_own[1]
    q1 = q1 + S1[2] * e3[1]

    @pl.when(first)
    def _():
        c1 = w0 + q0
        b = c1 + q1 + HALF * (local_rate(c1) - local_rate(w1))
        arrived(*r5)
        end = b + kc[1] * coarse_lap(d5[0] + e_own[0], c1 - w1, d5[2] + e_own[2])
        c5own[0] = end - c02[1]
        start(*r6)
        dd[1] = end - w2

    arrived(*r7)

    arrived(*r6)

    @pl.when(second)
    def _():
        d11, c11 = [], None
        for j in range(3):
            c10 = c5[j + 1] + c02[j]
            r = c10 + (a1p[j] + e_own[j]) + kc[j] * coarse_lap(c5[j], c5[j + 1], c5[j + 2]) + HALF * local_rate(c10)
            if j == 1:
                c11 = r + w1
            d11.append(r * m_out if j == 2 else r)
        end = c11 + q1 + kc[1] * coarse_lap(*d11) + HALF * (local_rate(c11) - local_rate(w1))
        dd[1] = end - w2

    up = prolong(dd[1])
    for p, plane in ((1, 1 - c), (2, c)):
        for sp, par in each():
            out_ref[0, sp, plane, pl.ds(par, 64, stride=2), :] = v2p[p, sp, par] + up[sp]

    for cond, cp in copies:
        when(cond, cp.wait_send)


def shards(n, initial, kappa):
    fine = lambda k: pltpu.VMEM((k, 2, 2, 64, 128), F32)
    coarse = lambda k: pltpu.VMEM((k, 64, 128), F32)
    return pl.pallas_call(
        functools.partial(kernel, n),
        out_shape=pltpu.VMEM((1,) + initial.shape, F32),
        in_specs=[pl.BlockSpec(memory_space=pltpu.HBM)] * 2,
        out_specs=pl.BlockSpec(memory_space=pltpu.VMEM),
        scratch_shapes=[
            pltpu.VMEM((5, 2, 128, 128), F32), pltpu.VMEM((4, 128, 128), F32),
            fine(5), fine(5), fine(5), fine(3), fine(3), fine(3), fine(3), fine(4), fine(4), fine(4), fine(3),
            coarse(5), coarse(3), coarse(3), coarse(2), coarse(2), coarse(5), coarse(3), coarse(2),
            pltpu.VMEM((2, 3, 2, 64, 128), F32), pltpu.VMEM((2, 3, 2, 2, 64, 128), F32),
            coarse(3), coarse(5), coarse(1), coarse(3), coarse(3),
            pltpu.SemaphoreType.DMA((4,)), pltpu.SemaphoreType.DMA((N_COPIES,)), pltpu.SemaphoreType.DMA((N_COPIES,)),
        ],
        compiler_params=pltpu.CompilerParams(
            collective_id=0, has_side_effects=True, vmem_limit_bytes=63 * 1024 * 1024),
    )(initial, kappa)


def solution(mesh):
    return jax.shard_map(
        functools.partial(shards, mesh.shape["space"]),
        mesh=mesh,
        in_specs=(P(None, "space", None, None), P("space", None, None)),
        out_specs=P("tm", None, "space", None, None),
        check_vma=False,
    )
```

```python
import functools

import jax
import jax.numpy as jnp
from jax import lax
from jax.experimental import pallas as pl
from jax.experimental.pallas import tpu as pltpu
from jax.sharding import PartitionSpec as P

MESH = pl.DeviceIdType.MESH
F32 = jnp.float32
STEP = 0.25
HALF = 0.125
FEED = 0.04
KILL = 0.06
S0 = (STEP * 5.0 / 24.0, STEP / 3.0, -STEP / 24.0)
S1 = (-STEP / 24.0, STEP / 3.0, STEP * 5.0 / 24.0)
N_COPIES = 48


def iota(dim):
    return lax.broadcasted_iota(jnp.int32, (64, 128), dim)


def even_lane():
    return iota(1) % 2 == 0


def beside_lanes(x, by):
    lane = iota(1)
    low = jnp.where(lane < by, 0.0, pltpu.roll(x, by, 1))
    high = jnp.where(lane >= 128 - by, 0.0, pltpu.roll(x, 128 - by, 1))
    return low + high


def row_above(x):
    return jnp.where(iota(0) == 0, 0.0, pltpu.roll(x, 1, 0))


def row_below(x):
    return jnp.where(iota(0) == 63, 0.0, pltpu.roll(x, 63, 0))


def kappas(kn, p):
    return [kn[p, pl.ds(par, 64, stride=2), :] for par in range(2)]


def fine_rate(buf, kn, p, below=True, above=True):
    centre = [[buf[p, sp, par] for par in range(2)] for sp in range(2)]
    kappa = kappas(kn, p)
    lap = []
    for sp in range(2):
        e, o = centre[sp]
        le = o + row_above(o) + beside_lanes(e, 1) - 6.0 * e
        lo = e + row_below(e) + beside_lanes(o, 1) - 6.0 * o
        for there, q in ((below, p - 1), (above, p + 1)):
            if there:
                le, lo = le + buf[q, sp, 0], lo + buf[q, sp, 1]
        lap.append((le, lo))
    out = [[None, None], [None, None]]
    for par in range(2):
        u, v = centre[0][par], centre[1][par]
        r = u * v * v
        out[0][par] = kappa[par] * lap[0][par] - r + FEED * (1.0 - u)
        out[1][par] = (0.5 * kappa[par]) * lap[1][par] + r - (FEED + KILL) * v
    return out


def across(buf, q, kn, p):
    return [[(k if sp == 0 else 0.5 * k) * buf[q, sp, par] for par, k in enumerate(kappas(kn, p))] for sp in range(2)]


def each():
    return [(sp, par) for sp in range(2) for par in range(2)]


def pairs(su, sv):
    return jnp.where(even_lane(), su + pltpu.roll(su, 127, 1), sv + pltpu.roll(sv, 1, 1))


def restrict(buf, a, b):
    s = [buf[a, sp, 0] + buf[a, sp, 1] + buf[b, sp, 0] + buf[b, sp, 1] for sp in range(2)]
    return 0.125 * pairs(s[0], s[1])


def restrict_plane(g):
    return 0.125 * pairs(g[0][0] + g[0][1], g[1][0] + g[1][1])


def prolong(d):
    even = even_lane()
    return jnp.where(even, d, pltpu.roll(d, 1, 1)), jnp.where(even, pltpu.roll(d, 127, 1), d)


def local_rate(c):
    even = even_lane()
    u, v = prolong(c)
    r = u * v * v
    return jnp.where(even, -r, r) - jnp.where(even, FEED, FEED + KILL) * c


def coarse_lap(below, d, above):
    return below + above + row_above(d) + row_below(d) + beside_lanes(d, 2) - 6.0 * d


def kernel(
    n, init_ref, kap_ref, out_ref,
    nat, kn, x0, x1, x2, f0, g1, g2, g0, base, ex, v1p, v2p,
    d1c, b2c, kc, wi, wpk, d11c, b11c, dd, pd, td, d5, c5, c5own, a1p, e3,
    lsem, ssem, rsem,
):
    me = lax.axis_index("space")
    t = lax.axis_index("tm")
    c = lax.rem(me, 2)
    partner = me + 1 - 2 * c
    outer = me - 1 + 2 * c
    far_in = me + 2 - 4 * c
    far_out = me - 2 + 4 * c
    has_out = jnp.logical_and(outer >= 0, outer < n)
    has_far = jnp.logical_and(far_in >= 0, far_in < n)
    always = None
    first, second = t == 0, t == 1
    def other_tm(other, rows, z, y):
        chip = other // 2 != me // 2
        row = jnp.logical_and(chip, other // 4 == me // 4)
        step_y = other // 16 != me // 16
        step_z = jnp.logical_and(other // 4 != me // 4, jnp.logical_not(step_y))
        turn = (other // 2) % 2 != (me // 2) % 2
        swap = jnp.zeros((), jnp.bool_)
        for wanted, there in ((rows, row), (z, jnp.logical_and(step_z, turn)), (y, step_y)):
            if wanted:
                swap = jnp.logical_or(swap, there)
        return jnp.where(swap, 1 - t, t)

    t_out, t_fin, t_fout = (other_tm(s, True, False, False) for s in (outer, far_in, far_out))
    t_inputs, t_late = other_tm(outer, True, True, False), other_tm(outer, True, False, True)

    m_out = jnp.where(has_out, 1.0, 0.0).astype(F32)

    def when(cond, fn):
        if cond is None:
            fn()
        else:
            pl.when(cond)(fn)

    def both(a, b):
        if a is None:
            return b
        return a if b is None else jnp.logical_and(a, b)

    copies = []

    def copy(src, dst, tm, space, cond, back="same"):
        i = len(copies)
        cp = pltpu.make_async_remote_copy(
            src_ref=src, dst_ref=dst, send_sem=ssem.at[i], recv_sem=rsem.at[i],
            device_id=(tm, space), device_id_type=MESH)
        copies.append((cond, cp))
        return cond, cond if isinstance(back, str) else back, cp

    def start(*cs):
        for cond, _, cp in cs:
            when(cond, cp.start)

    def arrived(*cs):
        for _, back, cp in cs:
            when(back, cp.wait_recv)

    barrier = pltpu.get_barrier_semaphore()
    around = [(has_out, far_out), (has_far, far_in), (has_out, outer), (always, partner)]
    greet = [(t, cond, s) for cond, s in around] + [(1 - t, cond, s) for cond, s in [(always, me)] + around]
    for tm, cond, s in greet:
        when(cond, lambda tm=tm, s=s: pl.semaphore_signal(barrier, inc=1, device_id=(tm, s), device_id_type=MESH))

    locals_ = [
        pltpu.make_async_copy(init_ref.at[:, 1 - c], nat.at[1], lsem.at[0]),
        pltpu.make_async_copy(init_ref.at[:, c], nat.at[2], lsem.at[1]),
        pltpu.make_async_copy(kap_ref.at[1 - c], kn.at[1], lsem.at[2]),
        pltpu.make_async_copy(kap_ref.at[c], kn.at[2], lsem.at[3]),
    ]
    for cp in locals_:
        cp.start()

    @pl.when(jnp.logical_not(has_out))
    def _():
        zero_plane = jnp.zeros((2, 2, 64, 128), F32)
        for buf in (x1, x2):
            buf[4] = zero_plane
        nat[3] = jnp.zeros((2, 128, 128), F32)
        nat[4] = jnp.zeros((2, 128, 128), F32)
        kn[3] = jnp.zeros((128, 128), F32)
        zero = jnp.zeros((64, 128), F32)
        for buf in (d1c, d11c, c5):
            buf[3] = zero
            buf[4] = zero
        for buf in (b2c, kc, b11c, d5, a1p):
            buf[2] = zero
        e3[1] = zero

    @pl.when(jnp.logical_not(has_far))
    def _():
        zero = jnp.zeros((64, 128), F32)
        for buf in (d1c, d11c, c5):
            buf[0] = zero
        e3[0] = zero

    pl.semaphore_wait(barrier, 3 + 4 * has_out.astype(jnp.int32) + 2 * has_far.astype(jnp.int32))

    for cp in locals_:
        cp.wait()
    p_init = copy(nat.at[1], nat.at[0], t, partner, always)
    o_init = copy(nat.at[2], nat.at[3], t_inputs, outer, has_out)
    p_kap = copy(kn.at[1], kn.at[0], t, partner, always)
    o_kap = copy(kn.at[2], kn.at[3], t_inputs, outer, has_out)
    o_init2 = copy(nat.at[1], nat.at[4], t_inputs, outer, has_out)
    start(p_init, o_init, o_kap, o_init2, p_kap)

    def convert(p):
        for sp, par in each():
            x0[p, sp, par] = nat[p, sp, pl.ds(par, 64, stride=2), :]

    convert(1)
    convert(2)
    ks = sum(kappas(kn, 1) + kappas(kn, 2))
    kc[1] = (0.125 * HALF / 4.0) * pairs(ks, 0.5 * ks)
    p_kc = copy(kc.at[1], kc.at[0], t, partner, always)
    o_kc = copy(kc.at[1], kc.at[2], t_late, outer, has_out)

    def masked(p):
        return jnp.where(p == 3, m_out, 1.0).astype(F32)

    def loop(lo, hi, body):
        def step(i, carry):
            body(i)
            return carry
        lax.fori_loop(lo, hi, step, 0)

    p_v1 = copy(x1.at[1], x1.at[0], t, partner, always)
    o_v1 = copy(x1.at[1], x1.at[4], t_out, outer, has_out)
    p_v2 = copy(x2.at[1], x2.at[0], t, partner, always)
    o_v2 = copy(x2.at[1], x2.at[4], t_late, outer, has_out)

    arrived(p_init)
    convert(0)

    def body_a1(p):
        @pl.when(p == 2)
        def _():
            arrived(o_init, o_kap, o_init2)
            convert(3)
            convert(4)

        f = fine_rate(x0, kn, p)
        m = masked(p)
        for sp, par in each():
            f0[p - 1, sp, par] = f[sp][par]
            x1[p, sp, par] = (x0[p, sp, par] + HALF * f[sp][par]) * m

        @pl.when(p == 1)
        def _():
            start(p_v1, o_v1)

    loop(1, 4, body_a1)

    def body_a2(p):
        @pl.when(p == 1)
        def _():
            arrived(p_v1)

        g = fine_rate(x1, kn, p)
        for sp, par in each():
            g1[p - 1, sp, par] = g[sp][par]
            x2[p, sp, par] = x1[p, sp, par] + HALF * g[sp][par]

        @pl.when(p == 1)
        def _():
            start(p_v2, p_kc, o_kc)

    loop(1, 3, body_a2)

    def store(dst, p, g):
        for sp, par in each():
            dst[p - 1, sp, par] = g[sp][par]

    store(g1, 3, fine_rate(x1, kn, 3, above=False))
    store(g2, 2, fine_rate(x2, kn, 2, above=False))
    w0, w1, w2 = (restrict(x, 1, 2) for x in (x0, x1, x2))
    rf, r1 = restrict(f0, 0, 1), restrict(g1, 0, 1)
    arrived(p_v2)
    store(g2, 1, fine_rate(x2, kn, 1))
    r2 = restrict(g2, 0, 1)
    q0 = S0[0] * rf + S0[1] * r1 + S0[2] * r2
    q1 = S1[0] * rf + S1[1] * r1 + S1[2] * r2

    arrived(o_v1)
    more = across(x1, 4, kn, 3)
    for sp, par in each():
        r = g1[2, sp, par] + more[sp][par]
        g1[2, sp, par] = r
        x2[3, sp, par] = (x1[3, sp, par] + HALF * r) * m_out
    more = across(x2, 3, kn, 2)
    for sp, par in each():
        g2[1, sp, par] = g2[1, sp, par] + more[sp][par]
    r2 = restrict_plane(more)
    q0 = q0 + S0[2] * r2
    q1 = q1 + S1[2] * r2
    c1 = w0 + q0
    d1c[2] = c1 - w1
    b2c[1] = c1 + q1 + HALF * (local_rate(c1) - local_rate(w1))
    wpk[0] = w0
    wpk[1] = w2

    def spread(buf, at, cond, t_out=t, t_fin=t, t_fout=t):
        return [
            copy(buf.at[at], buf.at[0], t_fout, far_out, both(cond, has_out), both(cond, has_far)),
            copy(buf.at[at], buf.at[4], t_fin, far_in, both(cond, has_far), both(cond, has_out)),
            copy(buf.at[at], buf.at[3], t_out, outer, both(cond, has_out)),
            copy(buf.at[at], buf.at[1], t, partner, cond),
        ]

    def beside(buf, cond, t_out=t):
        return [
            copy(buf.at[1], buf.at[2], t_out, outer, both(cond, has_out)),
            copy(buf.at[1], buf.at[0], t, partner, cond),
        ]

    round2 = spread(d1c, 2, always, t_out, t_fin, t_fout) + beside(b2c, always, t_out) + [copy(wpk, wi, t, partner, always)]
    start(*round2)
    start(o_v2)
    w0o = restrict(x0, 3, 4)
    arrived(p_kc, o_kc)

    def collect(p, start_at, f):
        for sp, par in each():
            a, b = g1[p - 1, sp, par], g2[p - 1, sp, par]
            base[p, sp, par] = start_at[sp][par] + S0[0] * f[sp][par] + S0[1] * a + S0[2] * b
            ex[p, sp, par] = S1[0] * f[sp][par] + (S1[1] - HALF) * a + S1[2] * b

    def fields(buf, p):
        return [[buf[p, sp, par] for par in range(2)] for sp in range(2)]

    def body_b1(p):
        collect(p, fields(x0, p), fields(f0, p - 1))

    loop(1, 3, body_b1)
    p_base = copy(base.at[1], base.at[0], t, partner, always)

    @pl.when(first)
    def _():
        start(p_base)

    arrived(*round2)
    w0s = (wi[0], w0, w0o)

    def corrected(d, b, j):
        r = b[j] + kc[j] * coarse_lap(d[j], d[j + 1], d[j + 2])
        return r * m_out if j == 2 else r

    c02 = [corrected(d1c, b2c, j) for j in range(3)]

    def correction(i, d):
        even = even_lane()
        lane = iota(1)
        for j in range(3):
            back, on, back2, on2 = (pltpu.roll(d[j], by, 1) for by in (1, 127, 2, 126))
            species = (
                (jnp.where(even, d[j], back), jnp.where(even, back2, on)),
                (jnp.where(even, on, d[j]), jnp.where(even, back, on2)),
            )
            for sp, (x, beside_x) in enumerate(species):
                pd[i, j, sp] = x
                t_ = jnp.where((lane == 0) | (lane == 127), 0.0, beside_x) - 3.0 * x
                td[i, j, sp, 0] = t_ + row_above(x)
                td[i, j, sp, 1] = t_ + row_below(x)

    def corrected_rate(i, src, p):
        own = (p + 1) // 2
        beyond = own + 1 - 2 * (p % 2)
        pu, pv = pd[i, own, 0], pd[i, own, 1]
        au, av = pd[i, beyond, 0], pd[i, beyond, 1]
        out = [[None, None], [None, None]]
        for par in range(2):
            k = kappas(kn, p)[par]
            u, v = src[p, 0, par], src[p, 1, par]
            un, vn = u + pu, v + pv
            r = un * vn * vn - u * v * v
            out[0][par] = k * (td[i, own, 0, par] + au) - r - FEED * pu
            out[1][par] = (0.5 * k) * (td[i, own, 1, par] + av) + r - (FEED + KILL) * pv
        return out

    r3 = spread(d11c, 2, second) + beside(b11c, second)

    @pl.when(second)
    def _():
        d10 = [c02[j] - w0s[j] for j in range(3)]
        c11 = c02[1] + q0 + kc[1] * coarse_lap(*d10) + HALF * (local_rate(c02[1]) - local_rate(w0))
        d11c[2] = c11 - w1
        b11c[1] = c11 + q1 + HALF * (local_rate(c11) - local_rate(w1))

    start(*r3)

    arrived(o_v2)
    w2s = (wi[1], w2, restrict(x2, 3, 4))
    store(g2, 3, fine_rate(x2, kn, 3))

    @pl.when(first)
    def _():
        body_b1(3)
        correction(0, [d1c[j + 1] for j in range(3)])
        correction(1, [c02[j] - w2s[j] for j in range(3)])

    @pl.when(second)
    def _():
        correction(0, [c02[j] - w0s[j] for j in range(3)])
        correction(1, [c02[j] - w2s[j] for j in range(3)])

        def body(p):
            df = corrected_rate(0, x0, p)
            dr = corrected_rate(1, x2, p)
            own = (p + 1) // 2
            y, f = fields(x2, p), fields(f0, p - 1)
            for sp, par in each():
                r = g2[p - 1, sp, par] + dr[sp][par]
                f[sp][par] = f[sp][par] + df[sp][par]
                g0[p - 1, sp, par] = r
                y[sp][par] = y[sp][par] + pd[1, own, sp] + HALF * (r - f[sp][par])
            collect(p, y, f)
        loop(1, 4, body)
        start(p_base)
        dd[0] = restrict(g0, 0, 1)

    @pl.when(first)
    def _():
        dd[0] = rf

    arrived(*r3)

    @pl.when(second)
    def _():
        correction(0, [d11c[j + 1] for j in range(3)])
        correction(1, [corrected(d11c, b11c, j) - w2s[j] for j in range(3)])

    p_v2p = copy(v2p.at[1], v2p.at[0], t, partner, always)
    r_e = [copy(e3.at[2], e3.at[0], t, far_out, has_out, has_far), copy(e3.at[2], e3.at[1], t, outer, has_out)]

    def second_node(p):
        g = fine_rate(v1p, kn, p)
        for sp, par in each():
            g1[p - 1, sp, par] = g[sp][par]
            v2p[p, sp, par] = v1p[p, sp, par] + ex[p, sp, par] + HALF * g[sp][par]

    arrived(p_base, p_kap)

    def body_c1(p):
        fa = corrected_rate(0, x1, p)
        fb = corrected_rate(1, x2, p)
        m = masked(p)
        for sp, par in each():
            a, b = fa[sp][par], fb[sp][par]
            v1p[p, sp, par] = (base[p, sp, par] + S0[1] * a + S0[2] * b) * m
            ex[p, sp, par] = ex[p, sp, par] + (S1[1] - HALF) * a + S1[2] * b

        @pl.when(p == 2)
        def _():
            second_node(1)
            start(p_v2p)

    loop(0, 4, body_c1)
    second_node(2)
    e3[2] = restrict_plane(across(v2p, 2, kn, 3))
    start(*r_e)
    store(g2, 2, fine_rate(v2p, kn, 2, above=False))
    store(g2, 1, fine_rate(v2p, kn, 1, below=False))

    w1, w2 = restrict(v1p, 1, 2), restrict(v2p, 1, 2)
    rf, r1, r2 = dd[0], restrict(g1, 0, 1), restrict(g2, 0, 1)
    q0 = S0[0] * rf + S0[1] * r1 + S0[2] * r2
    q1 = S1[0] * rf + S1[1] * r1 + S1[2] * r2
    arrived(p_v2p)
    r2 = restrict_plane(across(v2p, 0, kn, 1))
    q0 = q0 + S0[2] * r2
    q1 = q1 + S1[2] * r2

    r5 = beside(d5, first)
    r6 = [copy(c5own.at[0], c5.at[at], 1, s, both(first, cond), both(second, back))
          for at, cond, back, s in ((3, has_out, has_out, outer), (4, has_far, has_out, far_in),
                                    (0, has_out, has_far, far_out), (2, always, always, me),
                                    (1, always, always, partner))]
    r7 = beside(a1p, second)

    @pl.when(first)
    def _():
        d5[1] = w0 + q0 - w1
        start(*r5)

    @pl.when(second)
    def _():
        a1p[1] = q0 - HALF * local_rate(c02[1]) - w1
        start(*r7)

    arrived(*r_e)
    e_own = (S0[2] * e3[0], S0[2] * e3[1], S0[2] * e3[2])
    q0 = q0 + e_own[1]
    q1 = q1 + S1[2] * e3[1]

    @pl.when(first)
    def _():
        c1 = w0 + q0
        b = c1 + q1 + HALF * (local_rate(c1) - local_rate(w1))
        arrived(*r5)
        end = b + kc[1] * coarse_lap(d5[0] + e_own[0], c1 - w1, d5[2] + e_own[2])
        c5own[0] = end - c02[1]
        start(*r6)
        dd[1] = end - w2

    arrived(*r7)

    arrived(*r6)

    @pl.when(second)
    def _():
        d11, c11 = [], None
        for j in range(3):
            c10 = c5[j + 1] + c02[j]
            r = c10 + (a1p[j] + e_own[j]) + kc[j] * coarse_lap(c5[j], c5[j + 1], c5[j + 2]) + HALF * local_rate(c10)
            if j == 1:
                c11 = r + w1
            d11.append(r * m_out if j == 2 else r)
        end = c11 + q1 + kc[1] * coarse_lap(*d11) + HALF * (local_rate(c11) - local_rate(w1))
        dd[1] = end - w2

    up = prolong(dd[1])
    for p, plane in ((1, 1 - c), (2, c)):
        for sp, par in each():
            out_ref[0, sp, plane, pl.ds(par, 64, stride=2), :] = v2p[p, sp, par] + up[sp]

    for cond, cp in copies:
        when(cond, cp.wait_send)


def shards(n, initial, kappa):
    fine = lambda k: pltpu.VMEM((k, 2, 2, 64, 128), F32)
    coarse = lambda k: pltpu.VMEM((k, 64, 128), F32)
    return pl.pallas_call(
        functools.partial(kernel, n),
        out_shape=pltpu.VMEM((1,) + initial.shape, F32),
        in_specs=[pl.BlockSpec(memory_space=pltpu.HBM)] * 2,
        out_specs=pl.BlockSpec(memory_space=pltpu.VMEM),
        scratch_shapes=[
            pltpu.VMEM((5, 2, 128, 128), F32), pltpu.VMEM((4, 128, 128), F32),
            fine(5), fine(5), fine(5), fine(3), fine(3), fine(3), fine(3), fine(4), fine(4), fine(4), fine(3),
            coarse(5), coarse(3), coarse(3), coarse(2), coarse(2), coarse(5), coarse(3), coarse(2),
            pltpu.VMEM((2, 3, 2, 64, 128), F32), pltpu.VMEM((2, 3, 2, 2, 64, 128), F32),
            coarse(3), coarse(5), coarse(1), coarse(3), coarse(3),
            pltpu.SemaphoreType.DMA((4,)), pltpu.SemaphoreType.DMA((N_COPIES,)), pltpu.SemaphoreType.DMA((N_COPIES,)),
        ],
        compiler_params=pltpu.CompilerParams(
            collective_id=0, has_side_effects=True, vmem_limit_bytes=63 * 1024 * 1024),
    )(initial, kappa)


def solution(mesh):
    return jax.shard_map(
        functools.partial(shards, mesh.shape["space"]),
        mesh=mesh,
        in_specs=(P(None, "space", None, None), P("space", None, None)),
        out_specs=P("tm", None, "space", None, None),
        check_vma=False,
    )
```
